32 devices in a mesh: seq: 8 (over y, x, core), ep: 4 (over z).
Axes of the slice: x: 2, y: 2, z: 4, core: 2. Of those that a mesh axis runs over, the one named last changes fastest.
Arguments:
- tokens: bfloat16 [16384, 768], P('seq'), may hold values from -6 to 6
- input_proj: bfloat16 [768, 3, 768], P(None, None, 'ep'), may hold values from -0.21875 to 0.21875
- output_proj: bfloat16 [768, 768], P('ep'), may hold values from -0.21875 to 0.21875
- expert_index: int32 [16384, 1], P(('seq', 'ep')), may hold values from 0 to 31; in each aligned block of 512 rows (0 to 511, 512 to 1023, ...) at most 32 rows name the same one
- expert_in: bfloat16 [64, 768, 1536], P(('seq', 'ep')), may hold values from -0.21875 to 0.21875
- expert_out: bfloat16 [64, 1536, 768], P(('seq', 'ep')), may hold values from -0.109375 to 0.109375
Outputs:
- mixed_out: bfloat16 [16384, 768], P(('seq', 'ep'))
The draws below stay inside these ranges and needn't reach their ends.
Inputs may be any that keep to these rules, and one draw needn't show every extreme that they name: `expert_index`: among the rows of one device (aligned blocks of 512 rows) no expert is named more than 32 times, a bound that some block reaches.
All inputs are finite; a program needn't handle non-finite values.
Results may differ from the reference program's by a relative error of at most 0.015.
Values may be sent and summed in bfloat16 or wider, within the bound.
No kernel may reach another device: no remote copies, remote signals or barrier semaphores. Data moves between devices by JAX's collectives and lax.ppermute only.
A program may use at most 64 MiB of HBM per device.

```python
import math
import jax
import jax.numpy as jnp
import numpy as np
from jax import lax

D = 768
HEADS = 12
HD = 64
FF = 3072
EXP_DEV = 2
BLOCK = 512
TOKENS = 16384
ROWS_DEV = 512
EXPERTS = 32
FF_HALF = 1536
CAP = 32
N_SEQ = 8
N_EP = 4


def block_scale(own_key, dims, split, least, top_value):
    factor_of, own = 1.0, jax.random.fold_in(own_key, 6)
    for dim, blocks in split:
        heights = jnp.exp(jax.random.uniform(jax.random.fold_in(own, dim), (blocks,), jnp.float32, least / len(split), top_value / len(split)))
        factor_of = factor_of * jnp.repeat(heights, dims[dim] // blocks).reshape([-1 if axis == dim else 1 for axis in range(len(dims))])
    return factor_of


def routed_block(stream_key, own, number, rows, number_of, top, limit, slope):
    order = jax.random.permutation(stream_key, number_of)
    crowded, ordinary = shares(number_of, rows * top, limit, slope, True), shares(number_of, rows * top, limit, slope, False)
    places = jnp.arange(number_of)

    def named(tallies, rotation):
        used = int((tallies > 0).sum())
        fixed = max(1, used // 4)
        passed = fixed + (places - fixed + rotation * (used - fixed)) % max(1, number_of - fixed)
        return jnp.zeros((number_of,), jnp.int32).at[order[jnp.where(places < fixed, places, passed)]].set(jnp.asarray(tallies, jnp.int32))

    tallies = jnp.where(number % 4 == 0, named(crowded, number // 4), named(ordinary, number - number // 4 - 1))
    mixed = jax.random.permutation(jax.random.fold_in(own, 3), number_of)
    source_of, taker = mixed[0:number_of // 2 * 2:2], mixed[1:number_of // 2 * 2:2]
    room = jnp.minimum(tallies[source_of] - 1, limit - tallies[taker]) // 2
    room = jnp.where((source_of == order[0]) | (taker == order[0]) | (tallies[taker] == 0), 0, jnp.maximum(room, 0))
    passed = jax.random.randint(jax.random.fold_in(own, 4), (number_of // 2,), 0, 1 << 20) % (room + 1)
    tallies = tallies.at[source_of].add(-passed).at[taker].add(passed)
    items = jnp.searchsorted(jnp.cumsum(tallies), jnp.arange(rows * top), side="right").astype(jnp.int32)
    listing = items.reshape(top, rows).T
    listing = listing[jax.random.permutation(jax.random.fold_in(own, 1), rows)]
    rotation = jax.random.randint(jax.random.fold_in(own, 2), (rows, 1), 0, top)
    return jnp.take_along_axis(listing, (jnp.arange(top)[None, :] + rotation) % top, axis=1)


def shares(amount, total, limit, slope, full):
    portions = [(1 << 20) // math.isqrt(standing ** slope) + 1 for standing in range(1, amount + 1)]
    largest = limit if full else min(limit, max(-(-total // amount), total * portions[0] // sum(portions)))
    least = 1 if total - largest >= amount - 1 else 0
    given, rest = [largest] + [least] * (amount - 1), total - largest - least * (amount - 1)
    while rest > 0:
        movable = [i for i in range(1, amount) if given[i] < largest] or [i for i in range(1, amount) if given[i] < limit]
        mass, remaining = sum([portions[i] for i in movable]), rest
        for i in movable:
            addition = min(limit - given[i], max(1, remaining * portions[i] // mass), rest)
            given[i] = given[i] + addition
            rest = rest - addition
    return np.array(given)


def scatter_about(own_key, shape, spread, most, cuts=(), held_as=jnp.bfloat16):
    result = jax.random.normal(own_key, shape, jnp.float32) * spread
    if len(cuts) > 0:
        result = block_scale(own_key, shape, cuts, -0.22, 0.18) * result
    return jnp.clip(result, min=-most, max=most).astype(held_as)


def setup_inputs(seed: int = 0) -> dict:
    key_list = jax.random.split(jax.random.key(seed), 7)
    tokens = scatter_about(key_list[0], (TOKENS, D), 1.0, 6.0, ((0, 8),))
    input_proj = scatter_about(key_list[1], (D, 3, HEADS * HD), D ** -0.5, 0.21875, ((2, 4),))
    output_proj = scatter_about(key_list[2], (HEADS * HD, D), (HEADS * HD) ** -0.5, 0.21875, ((0, 4),))
    expert_index_keys = jax.random.split(jax.random.fold_in(key_list[3], 1), TOKENS // ROWS_DEV)
    expert_index_turns = jax.random.permutation(jax.random.fold_in(key_list[3], 3), TOKENS // ROWS_DEV)
    expert_index = jax.vmap(lambda own, number: routed_block(jax.random.fold_in(key_list[3], 2), own, number, ROWS_DEV, EXPERTS, 1, CAP, 1))(expert_index_keys, expert_index_turns).reshape((TOKENS, 1))
    expert_in = scatter_about(key_list[4], (2 * EXPERTS, D, FF_HALF), D ** -0.5, 0.21875, ((0, 32),))
    expert_out = scatter_about(key_list[5], (2 * EXPERTS, FF_HALF, D), FF ** -0.5, 0.109375, ((0, 32),))
    return {"tokens": tokens, "input_proj": input_proj, "output_proj": output_proj, "expert_index": expert_index, "expert_in": expert_in, "expert_out": expert_out}


epsilon = 1e-05

def rms_rows(values):
    return values * lax.rsqrt(lax.optimization_barrier(jnp.mean(values * values, axis=-1, keepdims=True)) + epsilon)

def attend_block(kv_state, block_rows):
    queries = block_rows[:, 0].astype(jnp.float32)
    key_rows = block_rows[:, 1].astype(jnp.float32)
    value_rows = block_rows[:, 2].astype(jnp.float32)
    scores = jnp.einsum('qhd,khd->hqk', queries, key_rows)
    causal = jnp.arange(BLOCK)[:, None] >= jnp.arange(BLOCK)[None, :]
    rounded = jnp.where(causal[None], scores, 0.0).astype(jnp.bfloat16)
    weights = lax.optimization_barrier(rounded).astype(jnp.float32)
    within = jnp.einsum('hqk,khd->qhd', weights, value_rows)
    across = jnp.einsum('qhd,hde->qhe', queries, kv_state, precision=lax.Precision.HIGHEST)
    block_out = rms_rows(across + within).astype(jnp.bfloat16).reshape(BLOCK, HEADS * HD)
    next_state = kv_state + jnp.einsum('khd,khe->hde', key_rows, value_rows)
    return (next_state, block_out)

def reference(tokens, input_proj, output_proj, expert_index, expert_in, expert_out):
    seq_total, model_width = tokens.shape
    normed = rms_rows(tokens.astype(jnp.float32)).astype(jnp.bfloat16)
    projected = jnp.dot(normed, input_proj.reshape(model_width, 3 * HEADS * HD), preferred_element_type=jnp.float32).astype(jnp.bfloat16)
    projected = lax.optimization_barrier(projected)
    projected = projected.reshape(seq_total // BLOCK, BLOCK, 3, HEADS, HD)
    start_state = jnp.zeros((HEADS, HD, HD), jnp.float32)
    final_state, heads_out = lax.scan(attend_block, start_state, projected)
    heads_out = heads_out.reshape(seq_total, HEADS * HD)
    group_cols = HEADS * HD // N_EP
    attn_out = jnp.zeros((seq_total, model_width), jnp.float32)
    for group_index in range(N_EP):
        lo_col = group_index * group_cols
        group_part = jnp.dot(heads_out[:, lo_col:lo_col + group_cols], output_proj[lo_col:lo_col + group_cols], preferred_element_type=jnp.float32).astype(jnp.bfloat16)
        attn_out = attn_out + lax.optimization_barrier(group_part).astype(jnp.float32)
    stream = (tokens.astype(jnp.float32) + attn_out).astype(jnp.bfloat16)
    stream = lax.optimization_barrier(stream)
    moe_in = rms_rows(stream.astype(jnp.float32)).astype(jnp.bfloat16)
    chosen = expert_index[:, 0].astype(jnp.int32)
    sort_order = jnp.argsort(chosen, stable=True).astype(jnp.int32)
    counts = jnp.zeros((EXPERTS,), jnp.int32).at[chosen].add(1)
    starts = (jnp.cumsum(counts) - counts).astype(jnp.int32)
    row_bound = N_SEQ * N_EP * CAP
    slots = jnp.arange(row_bound, dtype=jnp.int32)

    def one_expert(carried, expert):
        is_valid = slots < counts[expert]
        picked = sort_order[jnp.minimum(starts[expert] + slots, seq_total - 1)]
        rows_in = moe_in[picked]
        block_id = expert // EXP_DEV
        local_slot = expert % EXP_DEV
        total_part = jnp.zeros((row_bound, model_width), jnp.float32)
        for half_index in range(2):
            entry_row = ((2 * block_id + half_index) * EXP_DEV + local_slot).astype(jnp.int32)
            first_mat = lax.dynamic_index_in_dim(expert_in, entry_row, 0, keepdims=False)
            second_mat = lax.dynamic_index_in_dim(expert_out, entry_row, 0, keepdims=False)
            active = jnp.maximum(jnp.dot(rows_in, first_mat, preferred_element_type=jnp.float32), 0.0).astype(jnp.bfloat16)
            half_part = jnp.dot(active, second_mat, preferred_element_type=jnp.float32).astype(jnp.bfloat16)
            total_part = total_part + lax.optimization_barrier(half_part).astype(jnp.float32)
        moe_part = lax.optimization_barrier(total_part.astype(jnp.bfloat16)).astype(jnp.float32)
        carried = carried.at[picked].add(jnp.where(is_valid[:, None], moe_part, 0.0))
        return (carried, None)
    moe_out, scan_rest = lax.scan(one_expert, jnp.zeros((seq_total, model_width), jnp.float32), jnp.arange(EXPERTS, dtype=jnp.int32))
    return (stream.astype(jnp.float32) + moe_out).astype(jnp.bfloat16)
```

```python
import jax
import jax.numpy as jnp
from jax import lax
from jax.experimental import pallas as pl
from jax.experimental.pallas import tpu as pltpu
from jax.sharding import PartitionSpec as P

HD = 64
EXP_DEV = 2
BLOCK = 512
CHUNK = 256
SPLIT = 8
EPS = 1e-05
VMEM_BYTES = 48 * 1024 * 1024

F32 = jnp.float32
BF16 = jnp.bfloat16


def xor_pairs(count, bits):
    return [(place, place ^ bits) for place in range(count)]


def dot_nt(a, b):
    return lax.dot_general(a, b, (((1,), (1,)), ((), ())), preferred_element_type=F32)


def dot_tn(a, b):
    return lax.dot_general(a, b, (((0,), (0,)), ((), ())), preferred_element_type=F32)


def dot_nn(a, b):
    return jnp.dot(a, b, preferred_element_type=F32)


def two_terms(x):
    high = x.astype(BF16)
    return high, (x - high.astype(F32)).astype(BF16)


def rms(values):
    return values * lax.rsqrt(jnp.mean(values * values, axis=-1, keepdims=True) + EPS)


def same_head(width):
    rows = lax.broadcasted_iota(jnp.int32, (width, width), 0) // HD
    cols = lax.broadcasted_iota(jnp.int32, (width, width), 1) // HD
    return rows == cols


def params(semantics=1):
    return pltpu.CompilerParams(vmem_limit_bytes=VMEM_BYTES)


def cost(flops, nbytes):
    return pl.CostEstimate(flops=flops, bytes_accessed=nbytes, transcendentals=0)


def norm_states(tokens, stacked, width):
    rows, model = tokens.shape

    def kernel(tok_ref, w_ref, normed_ref, sum_ref, state):
        step = pl.program_id(0)

        @pl.when(step == 0)
        def _():
            state[...] = jnp.zeros_like(state)

        normed = rms(tok_ref[...].astype(F32)).astype(BF16)
        normed_ref[...] = normed
        keys = dot_nt(normed, w_ref[width : 2 * width, :]).astype(BF16)
        values = dot_nt(normed, w_ref[2 * width : 3 * width, :]).astype(BF16)
        state[...] += dot_tn(keys, values)

        @pl.when(step == pl.num_programs(0) - 1)
        def _():
            kept = jnp.where(same_head(width), state[...], 0.0)
            total = kept[:HD]
            for head in range(1, width // HD):
                total = total + kept[head * HD : (head + 1) * HD]
            sum_ref[...] = total.astype(BF16)

    return pl.pallas_call(
        kernel,
        grid=(rows // BLOCK,),
        in_specs=[
            pl.BlockSpec((BLOCK, model), lambda i: (i, 0)),
            pl.BlockSpec(stacked.shape, lambda i: (0, 0)),
        ],
        out_specs=[
            pl.BlockSpec((BLOCK, model), lambda i: (i, 0)),
            pl.BlockSpec((HD, width), lambda i: (0, 0)),
        ],
        out_shape=[
            jax.ShapeDtypeStruct((rows, model), BF16),
            jax.ShapeDtypeStruct((HD, width), BF16),
        ],
        scratch_shapes=[pltpu.VMEM((width, width), F32)],
        compiler_params=params(),
        cost_estimate=cost(2 * rows * model * 2 * width, 8 << 20),
    )(tokens, stacked)


def attend(meta, normed, pieces, prior, width):
    rows, model = normed.shape
    whole = len(pieces) == 1

    def kernel(meta_ref, normed_ref, *refs):
        piece_refs, prior_ref, out_ref = refs[: len(pieces)], refs[len(pieces)], refs[len(pieces) + 1]
        if whole:
            w_ref, state = piece_refs[0], refs[-1]
        else:
            proj_ref, w_ref, state = refs[-3:]
        step = pl.program_id(0)

        @pl.when(step == 0)
        def _():
            spread = jnp.concatenate([prior_ref[...].astype(F32)] * (width // HD), axis=0)
            state[...] = jnp.where(same_head(width), spread, 0.0)
            if not whole:
                part = pieces[0].shape[1]
                for parity in range(2):
                    for i in range(pieces[0].shape[0]):
                        place = (meta_ref[0] % SPLIT) ^ (2 * i + parity)
                        at = pl.ds(pl.multiple_of(place * part, part), part)
                        w_ref[at, :] = piece_refs[parity][i]
                proj_ref[...] = w_ref[3 * width : 4 * width, :]

        normed = normed_ref[...]
        queries = dot_nt(normed, w_ref[0:width, :]).astype(BF16)
        keys = dot_nt(normed, w_ref[width : 2 * width, :]).astype(BF16)
        values = dot_nt(normed, w_ref[2 * width : 3 * width, :]).astype(BF16)
        head_of = lax.broadcasted_iota(jnp.int32, (CHUNK, width), 1) // HD
        causal = lax.broadcasted_iota(jnp.int32, (CHUNK, CHUNK), 0) >= lax.broadcasted_iota(
            jnp.int32, (CHUNK, CHUNK), 1
        )
        heads_same = same_head(width)
        averaging = jnp.where(heads_same, 1.0 / HD, 0.0).astype(BF16)
        zero = jnp.zeros((), BF16)
        for c in range(BLOCK // CHUNK):
            q = queries[c * CHUNK : (c + 1) * CHUNK]
            k = keys[c * CHUNK : (c + 1) * CHUNK]
            v = values[c * CHUNK : (c + 1) * CHUNK]
            high, low = two_terms(state[...])
            attended = dot_nn(q, high) + dot_nn(q, low)
            for h in range(width // HD):
                scores = dot_nt(jnp.where(head_of == h, q, zero), k)
                weights = jnp.where(causal, scores, 0.0).astype(BF16)
                attended = attended + dot_nn(weights, jnp.where(head_of == h, v, zero))
            state[...] += jnp.where(heads_same, dot_tn(k, v), 0.0)
            high, low = two_terms(attended * attended)
            mean = dot_nn(high, averaging) + dot_nn(low, averaging)
            out_ref[c * CHUNK : (c + 1) * CHUNK, :] = (attended * lax.rsqrt(mean + EPS)).astype(BF16)

    def fixed(shape):
        return pl.BlockSpec(shape, lambda i, m: (0,) * len(shape))

    out_specs = [pl.BlockSpec((BLOCK, width), lambda i, m: (i, 0))]
    out_shape = [jax.ShapeDtypeStruct((rows, width), BF16)]
    scratch = [pltpu.VMEM((width, width), F32)]
    if not whole:
        out_specs.append(fixed((width, model)))
        out_shape.append(jax.ShapeDtypeStruct((width, model), BF16))
        scratch.insert(0, pltpu.VMEM((4 * width, model), BF16))
    return pl.pallas_call(
        kernel,
        grid_spec=pltpu.PrefetchScalarGridSpec(
            num_scalar_prefetch=1,
            grid=(rows // BLOCK,),
            in_specs=[pl.BlockSpec((BLOCK, model), lambda i, m: (i, 0))]
            + [fixed(p.shape) for p in pieces]
            + [fixed((HD, width))],
            out_specs=out_specs,
            scratch_shapes=scratch,
        ),
        out_shape=out_shape,
        compiler_params=params(),
        cost_estimate=cost(6 * rows * model * width, 6 << 20),
    )(meta, normed, *pieces, prior)


def slot_rows(chosen, experts, capacity):
    rows = chosen.shape[1]
    hot = chosen == lax.broadcasted_iota(jnp.int32, (experts, rows), 0)
    before = lax.broadcasted_iota(jnp.int32, (rows, rows), 0) < lax.broadcasted_iota(
        jnp.int32, (rows, rows), 1
    )
    preceding = dot_nn(hot.astype(BF16), before.astype(BF16))
    rank = jnp.sum(jnp.where(hot, preceding, 0.0), axis=0, keepdims=True)
    return chosen * capacity + rank.astype(jnp.int32)


def slot_cols(chosen, experts, capacity):
    rows = chosen.shape[0]
    hot = chosen == lax.broadcasted_iota(jnp.int32, (rows, experts), 1)
    before = lax.broadcasted_iota(jnp.int32, (rows, rows), 0) > lax.broadcasted_iota(
        jnp.int32, (rows, rows), 1
    )
    preceding = dot_nn(before.astype(BF16), hot.astype(BF16))
    rank = jnp.sum(jnp.where(hot, preceding, 0.0), axis=1, keepdims=True)
    return chosen * capacity + rank.astype(jnp.int32)


def pick(slots_row, moe_in, seq, ep, local, n_seq, n_ep, capacity):
    wanted = n_seq * capacity
    row = lax.broadcasted_iota(jnp.int32, (wanted, 1), 0)
    pair = ((row // capacity) ^ seq) * (n_ep // 2) + ep // 2
    key = (pair * EXP_DEV + local) * capacity + row % capacity
    hot = (key == slots_row).astype(BF16)
    return dot_nn(hot, moe_in).astype(BF16)


def route_first(meta, tokens, heads, projections, chosen, n_seq, n_ep, capacity, experts):
    rows, model = tokens.shape
    width = heads[0].shape[1]
    blocks = rows // BLOCK

    def kernel(meta_ref, tok_ref, idx_ref, *refs):
        head_refs, proj_refs = refs[:n_ep], refs[n_ep : 2 * n_ep]
        stream_ref, moe_ref, key_ref = refs[2 * n_ep : 2 * n_ep + 3]
        out_refs = refs[2 * n_ep + 3 :]
        total = tok_ref[...].astype(F32)
        for h_ref, p_ref in zip(head_refs, proj_refs):
            total = total + dot_nn(h_ref[...], p_ref[...])
        stream = total.astype(BF16)
        moe_in = rms(stream.astype(F32)).astype(BF16)
        moe_ref[0] = moe_in
        keys = slot_rows(idx_ref[0], experts, capacity)
        key_ref[0] = keys

        @pl.when(pl.program_id(0) == 0)
        def _():
            stream_ref[...] = stream

        picked = pick(keys, moe_in, meta_ref[0], meta_ref[1], 0, n_seq, n_ep, capacity)
        for k, out_ref in enumerate(out_refs):
            out_ref[0] = picked[k * capacity : (k + 1) * capacity]

    def fixed(shape):
        return pl.BlockSpec(shape, lambda i, m: (0,) * len(shape))

    at_block = lambda i, m: (i ^ m[1], 0)
    return pl.pallas_call(
        kernel,
        grid_spec=pltpu.PrefetchScalarGridSpec(
            num_scalar_prefetch=1,
            grid=(blocks,),
            in_specs=[
                pl.BlockSpec((BLOCK, model), at_block),
                pl.BlockSpec((1, 1, BLOCK), lambda i, m: (i ^ m[1], 0, 0)),
            ]
            + [pl.BlockSpec((BLOCK, width), at_block) for _ in heads]
            + [fixed(p.shape) for p in projections],
            out_specs=[
                fixed((BLOCK, model)),
                pl.BlockSpec((1, BLOCK, model), lambda i, m: (i, 0, 0)),
                pl.BlockSpec((1, 1, BLOCK), lambda i, m: (i, 0, 0)),
            ]
            + [pl.BlockSpec((1, capacity, model), lambda i, m: (i, 0, 0)) for _ in range(n_seq)],
        ),
        out_shape=[
            jax.ShapeDtypeStruct((BLOCK, model), BF16),
            jax.ShapeDtypeStruct((blocks, BLOCK, model), BF16),
            jax.ShapeDtypeStruct((blocks, 1, BLOCK), jnp.int32),
        ]
        + [jax.ShapeDtypeStruct((blocks, capacity, model), BF16) for _ in range(n_seq)],
        compiler_params=params(),
        cost_estimate=cost(2 * rows * model * model, 12 << 20),
    )(meta, tokens, chosen, *heads, *projections)


def route_next(meta, moe_in, keys, local, n_seq, n_ep, capacity):
    blocks, rows, model = moe_in.shape

    def kernel(meta_ref, moe_ref, key_ref, *out_refs):
        picked = pick(key_ref[0], moe_ref[0], meta_ref[0], meta_ref[1], local, n_seq, n_ep, capacity)
        for k, out_ref in enumerate(out_refs):
            out_ref[0] = picked[k * capacity : (k + 1) * capacity]

    return pl.pallas_call(
        kernel,
        grid_spec=pltpu.PrefetchScalarGridSpec(
            num_scalar_prefetch=1,
            grid=(blocks,),
            in_specs=[
                pl.BlockSpec((1, rows, model), lambda i, m: (i, 0, 0)),
                pl.BlockSpec((1, 1, rows), lambda i, m: (i, 0, 0)),
            ],
            out_specs=[pl.BlockSpec((1, capacity, model), lambda i, m: (i, 0, 0)) for _ in range(n_seq)],
        ),
        out_shape=[jax.ShapeDtypeStruct((blocks, capacity, model), BF16) for _ in range(n_seq)],
        compiler_params=params(),
        cost_estimate=cost(blocks * n_seq * capacity * rows * model * 2, 5 << 20),
    )(meta, moe_in, keys)


def expert(arrived, expert_in, expert_out, local):
    blocks, capacity, model = arrived[0].shape
    count = len(arrived)
    rows = blocks * count * capacity
    hidden = expert_in.shape[2]
    tile = 512
    steps = hidden // tile

    def kernel(*refs):
        in_refs, (w1, w2), out_refs, (held, total) = (
            refs[:count],
            refs[count : count + 2],
            refs[count + 2 : count + 2 + blocks],
            refs[count + 2 + blocks :],
        )
        step = pl.program_id(0)

        @pl.when(step == 0)
        def _():
            for k, ref in enumerate(in_refs):
                for m in range(blocks):
                    at = (m * count + k) * capacity
                    held[at : at + capacity, :] = ref[m]

        active = jnp.maximum(dot_nn(held[...], w1[0]), 0.0).astype(BF16)
        term = dot_nn(active, w2[0])

        @pl.when(step == 0)
        def _():
            total[...] = term

        @pl.when(step > 0)
        def _():
            total[...] += term

        @pl.when(step == steps - 1)
        def _():
            span = count * capacity
            for m, ref in enumerate(out_refs):
                ref[...] = total[m * span : (m + 1) * span, :].astype(BF16)

    return pl.pallas_call(
        kernel,
        grid=(steps,),
        in_specs=[pl.BlockSpec(a.shape, lambda f: (0, 0, 0)) for a in arrived]
        + [
            pl.BlockSpec((1, model, tile), lambda f: (local, 0, f)),
            pl.BlockSpec((1, tile, model), lambda f: (local, f, 0)),
        ],
        out_specs=[pl.BlockSpec((count * capacity, model), lambda f: (0, 0)) for _ in range(blocks)],
        out_shape=[jax.ShapeDtypeStruct((count * capacity, model), BF16) for _ in range(blocks)],
        scratch_shapes=[pltpu.VMEM((rows, model), BF16), pltpu.VMEM((rows, model), F32)],
        compiler_params=params(),
        cost_estimate=cost(4 * rows * model * hidden, 9 << 20),
    )(*arrived, expert_in, expert_out)


def add_halves(parts, n_seq, capacity):
    model = parts[0].shape[1]
    pairs = len(parts) // 2

    def kernel(*refs):
        in_refs, out_refs = refs[: len(parts)], refs[len(parts) :]
        for i in range(pairs):
            both = in_refs[2 * i][...].astype(F32) + in_refs[2 * i + 1][...].astype(F32)
            both = both.astype(BF16)
            for k in range(n_seq):
                out_refs[k][i * capacity : (i + 1) * capacity, :] = both[k * capacity : (k + 1) * capacity]

    return pl.pallas_call(
        kernel,
        out_shape=[jax.ShapeDtypeStruct((pairs * capacity, model), BF16) for _ in range(n_seq)],
        compiler_params=params(),
        cost_estimate=cost(1 << 20, 3 << 20),
    )(*parts)


def combine(meta, stream, chosen, returned, n_seq, n_ep, capacity, experts):
    rows, model = stream.shape
    pairs = n_ep // 2

    def kernel(meta_ref, stream_ref, idx_ref, *refs):
        out_ref = refs[-1]
        keys = slot_cols(idx_ref[...], experts, capacity)
        total = stream_ref[...].astype(F32)
        span = pairs * capacity
        col = lax.broadcasted_iota(jnp.int32, (1, n_seq * span), 1)
        seq = (col // span) ^ meta_ref[0]
        pair = seq * pairs + (((col // capacity) % pairs) ^ (meta_ref[1] // 2))
        for local in range(EXP_DEV):
            key = (pair * EXP_DEV + local) * capacity + col % capacity
            hot = (keys == key).astype(BF16)
            block = jnp.concatenate([r[...] for r in refs[local * n_seq : (local + 1) * n_seq]], axis=0)
            total = total + dot_nn(hot, block)
        out_ref[...] = total.astype(BF16)

    flat = [r for group in returned for r in group]
    return pl.pallas_call(
        kernel,
        in_specs=[pl.BlockSpec(memory_space=pltpu.SMEM)]
        + [pl.BlockSpec(memory_space=pltpu.VMEM)] * (2 + len(flat)),
        out_shape=jax.ShapeDtypeStruct((rows, model), BF16),
        compiler_params=params(),
        cost_estimate=cost(4 * rows * rows * model, 4 << 20),
    )(meta, stream, chosen, *flat)


def per_device(tokens, input_proj, output_proj, expert_index, expert_in, expert_out):
    rows, model = tokens.shape
    width = output_proj.shape[0]
    n_seq, n_ep = lax.axis_size("seq"), lax.axis_size("ep")
    seq, ep = lax.axis_index("seq"), lax.axis_index("ep")
    meta = jnp.stack([seq, ep]).astype(jnp.int32)
    own_rows = rows // n_ep
    experts = EXP_DEV * n_seq * n_ep // 2
    capacity = max(2, 2 * own_rows // experts)

    stacked = jnp.concatenate(
        [jnp.transpose(input_proj, (1, 2, 0)).reshape(3 * width, model), output_proj], axis=0
    )
    part = stacked.shape[0] // SPLIT
    piece = lax.dynamic_slice_in_dim(stacked, (seq % SPLIT) * part, part, 0)
    along = [None] + [lax.ppermute(piece, "ep", xor_pairs(n_ep, m)) for m in range(1, n_ep)]
    chosen_all = lax.all_gather(expert_index, "ep").reshape(n_ep, 1, own_rows)

    normed, own_sum = norm_states(tokens, stacked, width)
    sums = lax.all_gather(own_sum, "seq").astype(F32)
    earlier = (jnp.arange(n_seq) < seq).astype(F32)
    prior = jnp.sum(sums * earlier[:, None, None], axis=0).astype(BF16)
    priors = [prior] + [lax.ppermute(prior, "ep", xor_pairs(n_ep, m)) for m in range(1, n_ep)]

    heads, projections = [], []
    for m in range(n_ep):
        if m == 0:
            (out,) = attend(meta, normed, [stacked], priors[0], width)
            projections.append(output_proj)
        else:
            same = [along[m]] + [
                lax.ppermute(along[m], "seq", xor_pairs(n_seq, bits)) for bits in range(2, SPLIT, 2)
            ]
            same = jnp.stack(same)
            other = lax.ppermute(same, "seq", xor_pairs(n_seq, 1))
            out, proj = attend(meta, normed, [same, other], priors[m], width)
            projections.append(proj)
        heads.append(out)

    stream, moe_in, keys, *first = route_first(
        meta, tokens, heads, projections, chosen_all, n_seq, n_ep, capacity, experts
    )
    returned = []
    for local in range(EXP_DEV):
        outgoing = first if local == 0 else route_next(meta, moe_in, keys, local, n_seq, n_ep, capacity)
        arrived = [outgoing[0]] + [
            lax.ppermute(outgoing[k], "seq", xor_pairs(n_seq, k)) for k in range(1, n_seq)
        ]
        made = expert(arrived, expert_in, expert_out, local)
        parts = [made[0]] + [lax.ppermute(made[m], "ep", xor_pairs(n_ep, m)) for m in range(1, n_ep)]
        summed = add_halves(parts, n_seq, capacity)
        returned.append(
            [summed[0]] + [lax.ppermute(summed[k], "seq", xor_pairs(n_seq, k)) for k in range(1, n_seq)]
        )
    return combine(meta, stream, expert_index, returned, n_seq, n_ep, capacity, experts)


def solution(mesh):
    return jax.shard_map(
        per_device,
        mesh=mesh,
        in_specs=(
            P("seq", None),
            P(None, None, "ep"),
            P("ep", None),
            P(("seq", "ep"), None),
            P(("seq", "ep"), None, None),
            P(("seq", "ep"), None, None),
        ),
        out_specs=P(("seq", "ep"), None),
        check_vma=False,
    )
```

```python
import jax
import jax.numpy as jnp
from jax import lax
from jax.experimental import pallas as pl
from jax.experimental.pallas import tpu as pltpu
from jax.sharding import PartitionSpec as P

HD = 64
EXP_DEV = 2
BLOCK = 512
CHUNK = 256
SPLIT = 8
EPS = 1e-05
VMEM_BYTES = 40 * 1024 * 1024
EXPERT_VMEM_BYTES = 16 * 1024 * 1024
LANES = 128
FLOPS = 1.15e9
CELL = 256
CELLS = 26
NORMED, TOKENS, HEADS = 0, 3, 6

F32 = jnp.float32
BF16 = jnp.bfloat16


def xor_pairs(count, bits):
    return [(place, place ^ bits) for place in range(count)]


def dot_nt(a, b):
    return lax.dot_general(a, b, (((1,), (1,)), ((), ())), preferred_element_type=F32)


def dot_tn(a, b):
    return lax.dot_general(a, b, (((0,), (0,)), ((), ())), preferred_element_type=F32)


def dot_nn(a, b):
    return jnp.dot(a, b, preferred_element_type=F32)


def two_terms(x):
    high = x.astype(BF16)
    return high, (x - high.astype(F32)).astype(BF16)


def rms(values):
    return values * lax.rsqrt(jnp.mean(values * values, axis=-1, keepdims=True) + EPS)


def same_head(width):
    rows = lax.broadcasted_iota(jnp.int32, (width, width), 0) // HD
    cols = lax.broadcasted_iota(jnp.int32, (width, width), 1) // HD
    return rows == cols


def rows_of(i):
    return pl.ds(pl.multiple_of(i * BLOCK, BLOCK), BLOCK)


def call(kernel, out_shape, args, micros, scratch=(), space=None, reads=(), writes=(), steps=0, block=None, moving=None):
    given = [] if space is None else [space]
    rows = steps * BLOCK
    made = [] if not writes else [jax.ShapeDtypeStruct((CELLS, rows, CELL), BF16)]
    buffers = [pltpu.VMEM((rows, count * CELL), BF16) for _, count in (*reads, *writes)]
    sems = [pltpu.SemaphoreType.DMA((len(buffers), steps))] if buffers else []

    def body(*refs):
        ins, refs = refs[: len(args)], refs[len(args) :]
        given_ref, refs = refs[: len(given)], refs[len(given) :]
        outs, refs = refs[: len(out_shape)], refs[len(out_shape) :]
        made_ref, refs = refs[: len(made)], refs[len(made) :]
        own, held, sem = refs[: len(scratch)], refs[len(scratch) : len(scratch) + len(buffers)], refs[-1:]

        def copies(n, i):
            first, count = (*reads, *writes)[n]
            at = i if block is None or n >= moving else block(ins[0], i)
            there, here = rows_of(at), rows_of(i)
            for cell in range(count):
                near = held[n].at[here, pl.ds(cell * CELL, CELL)]
                if n < len(reads):
                    yield pltpu.make_async_copy(given_ref[0].at[first + cell, there], near, sem[0].at[n, i])
                else:
                    yield pltpu.make_async_copy(near, made_ref[0].at[first + cell, there], sem[0].at[n, i])

        def arrive(i, fixed=False):
            split = len(reads) if moving is None else moving
            for n in range(split, len(reads)) if fixed else range(split):
                for copy in copies(n, i):
                    copy.wait()

        def leave(i):
            for n in range(len(reads), len(buffers)):
                for copy in copies(n, i):
                    copy.start()

        if reads:

            @pl.loop(0, steps)
            def _(i):
                for n in range(len(reads)):
                    for copy in copies(n, i):
                        copy.start()

        kernel(ins, outs, own, arrive, leave, held[: len(reads)], held[len(reads) :])
        if writes:

            @pl.loop(0, steps)
            def _(i):
                for n in range(len(reads), len(buffers)):
                    for copy in copies(n, i):
                        copy.wait()

    return pl.pallas_call(
        body,
        in_specs=[pl.BlockSpec(memory_space=pltpu.SMEM)]
        + [pl.BlockSpec(memory_space=pltpu.VMEM)] * (len(args) - 1)
        + [pl.BlockSpec(memory_space=pl.ANY)] * len(given),
        out_specs=[pl.BlockSpec(memory_space=pltpu.VMEM)] * len(out_shape)
        + [pl.BlockSpec(memory_space=pl.ANY)] * len(made),
        out_shape=[jax.ShapeDtypeStruct(shape, dtype) for shape, dtype in out_shape] + made,
        scratch_shapes=[*scratch, *buffers, *sems],
        input_output_aliases={len(args): len(out_shape)} if given and made else {},
        compiler_params=pltpu.CompilerParams(vmem_limit_bytes=VMEM_BYTES),
        cost_estimate=pl.CostEstimate(flops=int(micros * FLOPS), bytes_accessed=1 << 20, transcendentals=0),
    )(*args, *given)


def attend_rows(normed, w_ref, width, state):
    q_all = dot_nt(normed, w_ref[0:width, :]).astype(BF16)
    k_all = dot_nt(normed, w_ref[width : 2 * width, :]).astype(BF16)
    v_all = dot_nt(normed, w_ref[2 * width : 3 * width, :]).astype(BF16)
    heads = width // HD
    head_of = lax.broadcasted_iota(jnp.int32, (CHUNK, width), 1) // HD
    causal = lax.broadcasted_iota(jnp.int32, (CHUNK, CHUNK), 0) >= lax.broadcasted_iota(
        jnp.int32, (CHUNK, CHUNK), 1
    )
    same = same_head(width)
    zero = jnp.zeros((), BF16)
    out = []
    for c in range(normed.shape[0] // CHUNK):
        q, k, v = (a[c * CHUNK : (c + 1) * CHUNK] for a in (q_all, k_all, v_all))
        attended = dot_nn(q, state.astype(BF16))
        stacked_q = jnp.concatenate([jnp.where(head_of == h, q, zero) for h in range(heads)], axis=0)
        scores = dot_nt(stacked_q, k)
        weights = jnp.concatenate(
            [jnp.where(causal, scores[h * CHUNK : (h + 1) * CHUNK], 0.0).astype(BF16) for h in range(heads)],
            axis=1,
        )
        stacked_v = jnp.concatenate([jnp.where(head_of == h, v, zero) for h in range(heads)], axis=0)
        out.append(attended + dot_nn(weights, stacked_v))
        state = state + jnp.where(same, dot_tn(k, v), 0.0)
    return q_all, jnp.concatenate(out, axis=0), state


def spread_heads(prior, width):
    spread = jnp.concatenate([prior] * (width // HD), axis=0)
    return jnp.where(same_head(width), spread, jnp.zeros((), prior.dtype))


def attend_own(meta, tokens, stacked, chosen, width, experts, capacity):
    rows, model = tokens.shape
    steps = rows // BLOCK

    def kernel(ins, outs, scratch, arrive, leave, reads, writes):
        _, w_ref, idx_ref, tok_ref = ins
        sum_ref, slot_ref = outs
        normed_ref, kept_ref, q_ref, att_ref = writes
        slot_ref[...] = slot_cols(idx_ref[...], experts, capacity)
        state = jnp.zeros((width, width), F32)
        for i in range(steps):
            at = slice(i * BLOCK, (i + 1) * BLOCK)
            kept_ref[at, :] = tok_ref[at, :]
            normed = rms(tok_ref[at, :].astype(F32)).astype(BF16)
            normed_ref[at, :] = normed
            q_ref[at, 0:width], attended, state = attend_rows(normed, w_ref, width, state)
            att_ref[at, 0:width] = attended.astype(BF16)
            leave(i)
        total = state[:HD]
        for head in range(1, width // HD):
            total = total + state[head * HD : (head + 1) * HD]
        sum_ref[...] = total.astype(BF16)

    cells = model // CELL
    return call(
        kernel,
        [((HD, width), BF16), (chosen.shape, jnp.int32)],
        [meta, stacked, chosen, tokens],
        7,
        writes=[(NORMED, cells), (TOKENS, cells), (HEADS, 1), (HEADS + 1, 1)],
        steps=steps,
    )


def place_slices(meta_ref, same_ref, other_ref, shard, w_ref):
    part = w_ref.shape[0] // SPLIT
    for parity, ref in enumerate((same_ref, other_ref)):
        for i in range(same_ref.shape[0]):
            place = (meta_ref[0] % SPLIT) ^ (2 * i + parity)
            at = pl.ds(pl.multiple_of(place * part, part), part)
            w_ref[at, :] = ref[i, shard * part : (shard + 1) * part]


def attend_other(meta, space, same, other, at_slice, shard, width, rows, model):
    steps = rows // BLOCK

    def kernel(ins, outs, scratch, arrive, leave, reads, writes):
        meta_ref, same_ref, other_ref = ins
        (normed_ref,), (q_ref, att_ref), (w_ref, state_ref) = reads, writes, scratch
        place_slices(meta_ref, same_ref, other_ref, at_slice, w_ref)
        outs[0][...] = w_ref[3 * width : 4 * width, :]
        state_ref[...] = jnp.zeros((width, width), F32)

        @pl.loop(0, steps, unroll=2)
        def _(i):
            at = rows_of(i)
            arrive(i)
            q_ref[at, 0:width], attended, state_ref[...] = attend_rows(
                normed_ref[at, :], w_ref, width, state_ref[...]
            )
            att_ref[at, 0:width] = attended.astype(BF16)
            leave(i)

    first = HEADS + 2 * shard
    return call(
        kernel,
        [((width, model), BF16)],
        [meta, same, other],
        8,
        [pltpu.VMEM((4 * width, model), BF16), pltpu.VMEM((width, width), F32)],
        space=space,
        reads=[(NORMED, model // CELL)],
        writes=[(first, 1), (first + 1, 1)],
        steps=steps,
    )


def slot_rows(chosen, experts, capacity):
    rows = chosen.shape[1]
    hot = chosen == lax.broadcasted_iota(jnp.int32, (experts, rows), 0)
    before = lax.broadcasted_iota(jnp.int32, (rows, rows), 0) < lax.broadcasted_iota(
        jnp.int32, (rows, rows), 1
    )
    preceding = dot_nn(hot.astype(BF16), before.astype(BF16))
    rank = jnp.sum(jnp.where(hot, preceding, 0.0), axis=0, keepdims=True)
    return chosen * capacity + rank.astype(jnp.int32)


def slot_cols(chosen, experts, capacity):
    rows = chosen.shape[0]
    hot = chosen == lax.broadcasted_iota(jnp.int32, (rows, experts), 1)
    before = lax.broadcasted_iota(jnp.int32, (rows, rows), 0) > lax.broadcasted_iota(
        jnp.int32, (rows, rows), 1
    )
    preceding = dot_nn(before.astype(BF16), hot.astype(BF16))
    rank = jnp.sum(jnp.where(hot, preceding, 0.0), axis=1, keepdims=True)
    return chosen * capacity + rank.astype(jnp.int32)


def pick(slots_row, moe_in, seq, ep, local, n_seq, n_ep, capacity):
    wanted = n_seq * capacity
    row = lax.broadcasted_iota(jnp.int32, (wanted, 1), 0)
    pair = ((row // capacity) ^ seq) * (n_ep // 2) + ep // 2
    key = (pair * EXP_DEV + local) * capacity + row % capacity
    hot = (key == slots_row).astype(BF16)
    return dot_nn(hot, moe_in).astype(BF16)


def route(meta, space, same, other, projections, priors, side, early_sum, rows, n_seq, n_ep, capacity, experts):
    width, model = projections[0].shape
    count = len(projections)
    half = rows // BLOCK // 2

    def block(meta_ref, i):
        return half * ((meta_ref[1] // 2) ^ side) + i

    def kernel(ins, outs, scratch, arrive, leave, reads, writes):
        meta_ref, same_ref, other_ref, *refs = ins
        prior_refs, proj_refs, refs = refs[:n_ep], refs[n_ep : n_ep + count], refs[n_ep + count :]
        w_ref, proj_ref, state_ref, key_ref = scratch
        (tok_ref, normed_ref, *kept), fixed = reads[: 2 + 2 * count], reads[2 + 2 * count :]
        place_slices(meta_ref, same_ref, other_ref, n_ep - 3, w_ref)
        for m in range(count):
            proj_ref[m * width : (m + 1) * width, :] = proj_refs[m][...]
        proj_ref[count * width : (count + 1) * width, :] = w_ref[3 * width : 4 * width, :]
        states = [spread_heads(ref[0:HD, :], width) for ref in prior_refs]
        averaging = jnp.where(same_head(width), 1.0 / HD, 0.0).astype(BF16)
        place = meta_ref[1]
        if early_sum is None:
            early, out_refs = jnp.zeros((width, width), F32), outs[1:]
            for i in range(half):
                arrive(i, True)
                n = fixed[0][i * BLOCK : (i + 1) * BLOCK, :]
                k = dot_nt(n, w_ref[width : 2 * width, :]).astype(BF16)
                v = dot_nt(n, w_ref[2 * width : 3 * width, :]).astype(BF16)
                early = early + dot_tn(k, v)
            early = jnp.where(same_head(width), early, 0.0)
            outs[0][...] = early
        else:
            early, out_refs = refs[0][...], outs[1:]
        second = ((place // 2) ^ side) == 1
        state_ref[...] = states[-1].astype(F32) + jnp.where(second, early, 0.0)
        for n in range(2):
            index = prior_refs[2 * side + n][HD : HD + BLOCK // LANES, 0:LANES].astype(F32).astype(jnp.int32)
            index = jnp.concatenate([index[r : r + 1] for r in range(BLOCK // LANES)], axis=1)
            key_ref[n] = slot_rows(index, experts, capacity)

        @pl.loop(0, half)
        def _(i):
            at = rows_of(i)
            relative = (place ^ i) % 2
            arrive(i)
            attended = [
                kept[2 * m + 1][at, 0:width].astype(F32) + dot_nn(kept[2 * m][at, 0:width], states[m])
                for m in range(count)
            ]
            _, last, state_ref[...] = attend_rows(normed_ref[at, :], w_ref, width, state_ref[...])
            heads = []
            for values in (*attended, last):
                mean = dot_nn((values * values).astype(BF16), averaging)
                heads.append((values * lax.rsqrt(mean + EPS)).astype(BF16))
            total = tok_ref[at, :].astype(F32) + dot_nn(jnp.concatenate(heads, axis=1), proj_ref[...])
            stream = total.astype(BF16)
            moe_in = rms(stream.astype(F32)).astype(BF16)
            if side == 0:

                @pl.when(relative == 0)
                def _():
                    outs[0][...] = stream

            for local in range(EXP_DEV):
                picked = pick(key_ref[relative], moe_in, meta_ref[0], place, local, n_seq, n_ep, capacity)
                for k in range(n_seq):
                    out_refs[k // 2][k % 2, relative, local] = picked[k * capacity : (k + 1) * capacity]

    extra = ((width, width), F32) if early_sum is None else ((BLOCK, model), BF16)
    cells = model // CELL
    parts = [(TOKENS, cells), (NORMED, cells)] + [(HEADS + n, 1) for n in range(2 * count)]
    return call(
        kernel,
        [extra] + [((2, 2, EXP_DEV, capacity, model), BF16)] * (n_seq // 2),
        [meta, same, other, *priors, *projections] + ([] if early_sum is None else [early_sum]),
        10,
        [pltpu.VMEM((4 * width, model), BF16), pltpu.VMEM(((count + 1) * width, model), BF16)]
        + [pltpu.VMEM((width, width), F32), pltpu.VMEM((2, 1, BLOCK), jnp.int32)],
        space=space,
        reads=parts + ([(NORMED, cells)] if early_sum is None else []),
        steps=half,
        block=block,
        moving=len(parts),
    )


def expert(got, crossed, expert_in, expert_out, local):
    _, blocks, _, capacity, model = got[0].shape
    count = len(got)
    span = 2 * count * capacity

    def kernel(*refs):
        got_refs, (crossed_ref, w1, w2), out_refs = refs[:count], refs[count : count + 3], refs[count + 3 :]
        pieces = []
        for n in range(blocks):
            for i in range(count):
                pieces += [got_refs[i][0, n, local], crossed_ref[i, n, local]]
        active = jnp.maximum(dot_nn(jnp.concatenate(pieces, axis=0), w1[local]), 0.0).astype(BF16)
        made = dot_nn(active, w2[local]).astype(BF16)
        for n in range(blocks):
            out_refs[n][...] = made[n * span : (n + 1) * span]

    return pl.pallas_call(
        kernel,
        in_specs=[pl.BlockSpec(memory_space=pltpu.VMEM)] * (count + 3),
        out_specs=[pl.BlockSpec(memory_space=pltpu.VMEM)] * blocks,
        out_shape=[jax.ShapeDtypeStruct((span, model), BF16)] * blocks,
        compiler_params=pltpu.CompilerParams(vmem_limit_bytes=EXPERT_VMEM_BYTES),
        cost_estimate=pl.CostEstimate(flops=int(5 * FLOPS), bytes_accessed=1 << 20, transcendentals=0),
    )(*got, crossed, expert_in, expert_out)


def lay_out(meta, own, half, other, n_seq, capacity):
    model = own.shape[1]

    def kernel(ins, outs, scratch, arrive, leave, reads, writes):
        _, own_ref, half_ref, other_ref = ins
        both = (own_ref[...].astype(F32) + half_ref[...].astype(F32)).astype(BF16)
        for side, rows in enumerate((both, other_ref[...])):
            for k in range(n_seq):
                outs[k // 2][k % 2, side * capacity : (side + 1) * capacity, :] = rows[k * capacity : (k + 1) * capacity]

    return call(
        kernel, [((2, 2 * capacity, model), BF16)] * (n_seq // 2), [meta, own, half, other], 0.6
    )


def combine(meta, stream, slots, returned, n_seq, n_ep, capacity):
    rows, model = stream.shape
    count = n_seq // 2 + 1

    def kernel(ins, outs, scratch, arrive, leave, reads, writes):
        meta_ref, stream_ref, slot_ref, *refs = ins
        keys = slot_ref[...]
        total = stream_ref[...].astype(F32)
        span = 2 * capacity
        col = lax.broadcasted_iota(jnp.int32, (1, n_seq * span), 1)
        seq = (col // span) ^ meta_ref[0]
        pair = seq * (n_ep // 2) + ((col // capacity) % 2 ^ (meta_ref[1] // 2))
        for local in range(EXP_DEV):
            key = (pair * EXP_DEV + local) * capacity + col % capacity
            hot = (keys == key).astype(BF16)
            *got_refs, crossed_ref = refs[local * count : (local + 1) * count]
            pieces = []
            for i, got_ref in enumerate(got_refs):
                pieces += [got_ref[0], crossed_ref[i]]
            total = total + dot_nn(hot, jnp.concatenate(pieces, axis=0))
        outs[0][...] = total.astype(BF16)

    flat = [r for got, crossed in returned for r in (*got, crossed)]
    return call(kernel, [((rows, model), BF16)], [meta, stream, slots, *flat], 2.5)[0]


def per_device(tokens, input_proj, output_proj, expert_index, expert_in, expert_out):
    rows, model = tokens.shape
    width = output_proj.shape[0]
    n_seq, n_ep = lax.axis_size("seq"), lax.axis_size("ep")
    seq, ep = lax.axis_index("seq"), lax.axis_index("ep")
    meta = jnp.stack([seq, ep]).astype(jnp.int32)
    own_rows = rows // n_ep
    experts = EXP_DEV * n_seq * n_ep // 2
    capacity = max(2, 2 * own_rows // experts)

    def over_seq(x, bits):
        return lax.ppermute(x, "seq", xor_pairs(n_seq, bits)) if bits else x

    def over_ep(x, bits):
        return lax.ppermute(x, "ep", xor_pairs(n_ep, bits)) if bits else x

    def exchange(outgoing, after=()):
        got = [over_seq(out, 2 * i) for i, out in enumerate(outgoing)]
        got, after = lax.optimization_barrier((got, after))
        return got, over_seq(jnp.stack([g[1] for g in got]), 1)

    stacked = jnp.concatenate(
        [jnp.transpose(input_proj, (1, 2, 0)).reshape(3 * width, model), output_proj], axis=0
    )
    part = stacked.shape[0] // SPLIT
    along = [lax.dynamic_slice_in_dim(stacked, (seq % SPLIT) * part, part, 0)]
    for bit in range(n_ep.bit_length() - 1):
        along.append(over_ep(along[0], 1 << bit))

    own_sum, slots, space = attend_own(
        meta, tokens, stacked, expert_index, width, experts, capacity
    )
    along, own_sum = lax.optimization_barrier((along, own_sum))
    along = {0: along[0], **{1 << bit: a for bit, a in enumerate(along[1:])}}
    for m in range(1, n_ep):
        low = m & (m - 1)
        if low:
            along[m] = over_ep(along[low], m ^ low)

    def gather_layer(pieces):
        first = jnp.concatenate(pieces, axis=0)
        return [over_seq(first, bits) for bits in range(0, SPLIT, 2)]

    early = gather_layer([along[1], own_sum.reshape(-1, model)])
    later = [along[m] for m in range(2, n_ep)]
    later, early = lax.optimization_barrier((later, early))
    late = gather_layer(later)
    early = jnp.stack(early)
    early_other = over_seq(early, 1)

    sum_rows = own_sum.size // model
    sums = jnp.stack([early[:, -sum_rows:], early_other[:, -sum_rows:]], axis=1).reshape(SPLIT, HD, width)
    earlier = (jnp.arange(SPLIT) ^ (seq % SPLIT)) < seq % SPLIT
    prior = jnp.sum(jnp.where(earlier[:, None, None], sums.astype(F32), 0.0), axis=0)
    total, bit = jnp.sum(sums.astype(F32), axis=0), SPLIT
    while bit < n_seq:
        arrived = over_seq(total.astype(BF16), bit).astype(F32)
        prior = prior + jnp.where((seq & bit) != 0, arrived, 0.0)
        total, bit = total + arrived, 2 * bit
    index_rows = jnp.pad(
        expert_index.astype(BF16).reshape(own_rows // LANES, LANES), ((0, 4), (0, width - LANES))
    )
    prior = jnp.concatenate([prior.astype(BF16), index_rows], axis=0)
    priors = [over_ep(prior, m) for m in range(n_ep)]

    early, prior = lax.optimization_barrier((early, prior))
    proj, space = attend_other(meta, space, early, early_other, 0, 1, width, rows, model)
    projections = [output_proj, proj]
    late, projections, priors = lax.optimization_barrier((late, projections, priors))
    late = jnp.stack(late)
    late_other = over_seq(late, 1)
    for m in range(2, n_ep - 1):
        proj, space = attend_other(meta, space, late, late_other, m - 2, m, width, rows, model)
        projections.append(proj)

    def send(side, early_sum):
        return route(
            meta, space, late, late_other, projections, priors, side, early_sum, rows, n_seq, n_ep, capacity, experts
        )

    early_sum, *outgoing = send(1, None)
    stream, *outgoing_own = send(0, early_sum)
    got, crossed = exchange(outgoing, outgoing_own)
    outgoing_own, got = lax.optimization_barrier((outgoing_own, got))
    made, halves = [], []
    for local in range(EXP_DEV):
        if made:
            crossed, made = lax.optimization_barrier((crossed, made))
        made.append(expert(got, crossed, expert_in, expert_out, local))
        halves.append(over_ep(made[-1][1], 1))
    sums = [(pair[0].astype(F32) + half.astype(F32)).astype(BF16) for pair, half in zip(made, halves)]
    got, crossed = exchange(outgoing_own, sums)
    others = [over_ep(both, 2) for both in sums]
    returned = []
    for local in range(EXP_DEV):
        if local > 0:
            crossed, others[0] = lax.optimization_barrier((crossed, others[0]))
        own = expert(got, crossed, expert_in, expert_out, local)
        parts = (own[0], over_ep(own[1], 1), others[local])
        if returned:
            parts, returned[-1] = lax.optimization_barrier((parts, returned[-1]))
        returned.append(exchange(lay_out(meta, *parts, n_seq, capacity)))
    return combine(meta, stream, slots, returned, n_seq, n_ep, capacity)


def solution(mesh):
    return jax.shard_map(
        per_device,
        mesh=mesh,
        in_specs=(
            P("seq", None),
            P(None, None, "ep"),
            P("ep", None),
            P(("seq", "ep"), None),
            P(("seq", "ep"), None, None),
            P(("seq", "ep"), None, None),
        ),
        out_specs=P(("seq", "ep"), None),
        check_vma=False,
    )
```

```python
import jax
import jax.numpy as jnp
from jax import lax
from jax.experimental import pallas as pl
from jax.experimental.pallas import tpu as pltpu
from jax.sharding import PartitionSpec as P

HD = 64
EXP_DEV = 2
BLOCK = 512
CHUNK = 256
SPLIT = 8
EPS = 1e-05
VMEM_BYTES = 40 * 1024 * 1024
EXPERT_VMEM_BYTES = 16 * 1024 * 1024
LANES = 128
FLOPS = 1.15e9
CELL = 256
CELLS = 26
NORMED, TOKENS, HEADS = 0, 3, 6

F32 = jnp.float32
BF16 = jnp.bfloat16


def xor_pairs(count, bits):
    return [(place, place ^ bits) for place in range(count)]


def dot_nt(a, b):
    return lax.dot_general(a, b, (((1,), (1,)), ((), ())), preferred_element_type=F32)


def dot_tn(a, b):
    return lax.dot_general(a, b, (((0,), (0,)), ((), ())), preferred_element_type=F32)


def dot_nn(a, b):
    return jnp.dot(a, b, preferred_element_type=F32)


def two_terms(x):
    high = x.astype(BF16)
    return high, (x - high.astype(F32)).astype(BF16)


def rms(values):
    return values * lax.rsqrt(jnp.mean(values * values, axis=-1, keepdims=True) + EPS)


def same_head(width):
    rows = lax.broadcasted_iota(jnp.int32, (width, width), 0) // HD
    cols = lax.broadcasted_iota(jnp.int32, (width, width), 1) // HD
    return rows == cols


def rows_of(i):
    return pl.ds(pl.multiple_of(i * BLOCK, BLOCK), BLOCK)


def call(kernel, out_shape, args, micros, scratch=(), space=None, reads=(), writes=(), steps=0, block=None, moving=None):
    given = [] if space is None else [space]
    rows = steps * BLOCK
    made = [] if not writes else [jax.ShapeDtypeStruct((CELLS, rows, CELL), BF16)]
    buffers = [pltpu.VMEM((rows, count * CELL), BF16) for _, count in (*reads, *writes)]
    sems = [pltpu.SemaphoreType.DMA((len(buffers), steps))] if buffers else []

    def body(*refs):
        ins, refs = refs[: len(args)], refs[len(args) :]
        given_ref, refs = refs[: len(given)], refs[len(given) :]
        outs, refs = refs[: len(out_shape)], refs[len(out_shape) :]
        made_ref, refs = refs[: len(made)], refs[len(made) :]
        own, held, sem = refs[: len(scratch)], refs[len(scratch) : len(scratch) + len(buffers)], refs[-1:]

        def copies(n, i):
            first, count = (*reads, *writes)[n]
            at = i if block is None or n >= moving else block(ins[0], i)
            there, here = rows_of(at), rows_of(i)
            for cell in range(count):
                near = held[n].at[here, pl.ds(cell * CELL, CELL)]
                if n < len(reads):
                    yield pltpu.make_async_copy(given_ref[0].at[first + cell, there], near, sem[0].at[n, i])
                else:
                    yield pltpu.make_async_copy(near, made_ref[0].at[first + cell, there], sem[0].at[n, i])

        split = len(reads) if moving is None else moving

        def fetch(i, parts):
            for n in parts:
                for copy in copies(n, i):
                    copy.start()

        def arrive(i, fixed=False):
            parts = range(split, len(reads)) if fixed else range(split)
            for n in parts:
                for copy in copies(n, i):
                    copy.wait()
            if not fixed:

                @pl.when(i + 1 < steps)
                def _():
                    fetch(i + 1, parts)

        def leave(i):
            for n in range(len(reads), len(buffers)):
                for copy in copies(n, i):
                    copy.start()

        if reads:
            for i in range(steps):
                fetch(i, range(split, len(reads)))
            fetch(0, range(split))
        kernel(ins, outs, own, arrive, leave, held[: len(reads)], held[len(reads) :])
        if writes:

            @pl.loop(0, steps)
            def _(i):
                for n in range(len(reads), len(buffers)):
                    for copy in copies(n, i):
                        copy.wait()

    return pl.pallas_call(
        body,
        in_specs=[pl.BlockSpec(memory_space=pltpu.SMEM)]
        + [pl.BlockSpec(memory_space=pltpu.VMEM)] * (len(args) - 1)
        + [pl.BlockSpec(memory_space=pl.ANY)] * len(given),
        out_specs=[pl.BlockSpec(memory_space=pltpu.VMEM)] * len(out_shape)
        + [pl.BlockSpec(memory_space=pl.ANY)] * len(made),
        out_shape=[jax.ShapeDtypeStruct(shape, dtype) for shape, dtype in out_shape] + made,
        scratch_shapes=[*scratch, *buffers, *sems],
        input_output_aliases={len(args): len(out_shape)} if given and made else {},
        compiler_params=pltpu.CompilerParams(vmem_limit_bytes=VMEM_BYTES),
        cost_estimate=pl.CostEstimate(flops=int(micros * FLOPS), bytes_accessed=1 << 20, transcendentals=0),
    )(*args, *given)


def attend_rows(normed, w_ref, width, state):
    q_all = dot_nt(normed, w_ref[0:width, :]).astype(BF16)
    k_all = dot_nt(normed, w_ref[width : 2 * width, :]).astype(BF16)
    v_all = dot_nt(normed, w_ref[2 * width : 3 * width, :]).astype(BF16)
    heads = width // HD
    head_of = lax.broadcasted_iota(jnp.int32, (CHUNK, width), 1) // HD
    causal = lax.broadcasted_iota(jnp.int32, (CHUNK, CHUNK), 0) >= lax.broadcasted_iota(
        jnp.int32, (CHUNK, CHUNK), 1
    )
    same = same_head(width)
    zero = jnp.zeros((), BF16)
    out = []
    for c in range(normed.shape[0] // CHUNK):
        q, k, v = (a[c * CHUNK : (c + 1) * CHUNK] for a in (q_all, k_all, v_all))
        attended = dot_nn(q, state.astype(BF16))
        stacked_q = jnp.concatenate([jnp.where(head_of == h, q, zero) for h in range(heads)], axis=0)
        scores = dot_nt(stacked_q, k)
        weights = jnp.concatenate(
            [jnp.where(causal, scores[h * CHUNK : (h + 1) * CHUNK], 0.0).astype(BF16) for h in range(heads)],
            axis=1,
        )
        stacked_v = jnp.concatenate([jnp.where(head_of == h, v, zero) for h in range(heads)], axis=0)
        out.append(attended + dot_nn(weights, stacked_v))
        state = state + jnp.where(same, dot_tn(k, v), 0.0)
    return q_all, jnp.concatenate(out, axis=0), state


def spread_heads(prior, width):
    spread = jnp.concatenate([prior] * (width // HD), axis=0)
    return jnp.where(same_head(width), spread, jnp.zeros((), prior.dtype))


def attend_own(meta, tokens, stacked, chosen, width, experts, capacity):
    rows, model = tokens.shape
    steps = rows // BLOCK

    def kernel(ins, outs, scratch, arrive, leave, reads, writes):
        _, w_ref, idx_ref, tok_ref = ins
        sum_ref, slot_ref = outs
        normed_ref, kept_ref, q_ref, att_ref = writes
        slot_ref[...] = slot_cols(idx_ref[...], experts, capacity)
        state = jnp.zeros((width, width), F32)
        for i in range(steps):
            at = slice(i * BLOCK, (i + 1) * BLOCK)
            kept_ref[at, :] = tok_ref[at, :]
            normed = rms(tok_ref[at, :].astype(F32)).astype(BF16)
            normed_ref[at, :] = normed
            q_ref[at, 0:width], attended, state = attend_rows(normed, w_ref, width, state)
            att_ref[at, 0:width] = attended.astype(BF16)
            leave(i)
        total = state[:HD]
        for head in range(1, width // HD):
            total = total + state[head * HD : (head + 1) * HD]
        sum_ref[...] = total.astype(BF16)

    cells = model // CELL
    return call(
        kernel,
        [((HD, width), BF16), (chosen.shape, jnp.int32)],
        [meta, stacked, chosen, tokens],
        7,
        writes=[(NORMED, cells), (TOKENS, cells), (HEADS, 1), (HEADS + 1, 1)],
        steps=steps,
    )


def place_slices(meta_ref, same_ref, other_ref, shard, w_ref):
    part = w_ref.shape[0] // SPLIT
    for parity, ref in enumerate((same_ref, other_ref)):
        for i in range(same_ref.shape[0]):
            place = (meta_ref[0] % SPLIT) ^ (2 * i + parity)
            at = pl.ds(pl.multiple_of(place * part, part), part)
            w_ref[at, :] = ref[i, shard * part : (shard + 1) * part]


def attend_other(meta, space, same, other, shard, width, rows, model):
    steps = rows // BLOCK

    def kernel(ins, outs, scratch, arrive, leave, reads, writes):
        meta_ref, same_ref, other_ref = ins
        (normed_ref,), (q_ref, att_ref), (w_ref, state_ref) = reads, writes, scratch
        place_slices(meta_ref, same_ref, other_ref, 0, w_ref)
        outs[0][...] = w_ref[3 * width : 4 * width, :]
        state_ref[...] = jnp.zeros((width, width), F32)

        @pl.loop(0, steps, unroll=2)
        def _(i):
            at = rows_of(i)
            arrive(i)
            q_ref[at, 0:width], attended, state_ref[...] = attend_rows(
                normed_ref[at, :], w_ref, width, state_ref[...]
            )
            att_ref[at, 0:width] = attended.astype(BF16)
            leave(i)

    first = HEADS + 2 * shard
    return call(
        kernel,
        [((width, model), BF16)],
        [meta, same, other],
        8,
        [pltpu.VMEM((4 * width, model), BF16), pltpu.VMEM((width, width), F32)],
        space=space,
        reads=[(NORMED, model // CELL)],
        writes=[(first, 1), (first + 1, 1)],
        steps=steps,
    )


def slot_rows(chosen, experts, capacity):
    rows = chosen.shape[1]
    hot = chosen == lax.broadcasted_iota(jnp.int32, (experts, rows), 0)
    before = lax.broadcasted_iota(jnp.int32, (rows, rows), 0) < lax.broadcasted_iota(
        jnp.int32, (rows, rows), 1
    )
    preceding = dot_nn(hot.astype(BF16), before.astype(BF16))
    rank = jnp.sum(jnp.where(hot, preceding, 0.0), axis=0, keepdims=True)
    return chosen * capacity + rank.astype(jnp.int32)


def slot_cols(chosen, experts, capacity):
    rows = chosen.shape[0]
    hot = chosen == lax.broadcasted_iota(jnp.int32, (rows, experts), 1)
    before = lax.broadcasted_iota(jnp.int32, (rows, rows), 0) > lax.broadcasted_iota(
        jnp.int32, (rows, rows), 1
    )
    preceding = dot_nn(before.astype(BF16), hot.astype(BF16))
    rank = jnp.sum(jnp.where(hot, preceding, 0.0), axis=1, keepdims=True)
    return chosen * capacity + rank.astype(jnp.int32)


def pick(slots_row, moe_in, seq, ep, local, n_seq, n_ep, capacity):
    wanted = n_seq * capacity
    row = lax.broadcasted_iota(jnp.int32, (wanted, 1), 0)
    pair = ((row // capacity) ^ seq) * (n_ep // 2) + ep // 2
    key = (pair * EXP_DEV + local) * capacity + row % capacity
    hot = (key == slots_row).astype(BF16)
    return dot_nn(hot, moe_in).astype(BF16)


def route(meta, space, same, other, projections, priors, side, early_sum, rows, n_seq, n_ep, capacity, experts):
    width, model = projections[0].shape
    count = len(projections)
    lasts = n_ep - count
    half = rows // BLOCK // 2

    def block(meta_ref, i):
        return half * ((meta_ref[1] // 2) ^ side) + i

    def kernel(ins, outs, scratch, arrive, leave, reads, writes):
        meta_ref, same_ref, other_ref, *refs = ins
        prior_refs, proj_refs, refs = refs[:n_ep], refs[n_ep : n_ep + count], refs[n_ep + count :]
        proj_ref, state_ref, key_ref, *w_refs = scratch
        (tok_ref, normed_ref, *kept), fixed = reads[: 2 + 2 * count], reads[2 + 2 * count :]
        for m in range(count):
            proj_ref[m * width : (m + 1) * width, :] = proj_refs[m][...]
        for n, w_ref in enumerate(w_refs):
            m = count + n
            place_slices(meta_ref, same_ref, other_ref, n, w_ref)
            proj_ref[m * width : (m + 1) * width, :] = w_ref[3 * width : 4 * width, :]
        same_heads = same_head(width)
        states = [spread_heads(ref[0:HD, :], width) for ref in prior_refs]
        averaging = jnp.where(same_heads, 1.0 / HD, 0.0).astype(BF16)
        place = meta_ref[1]
        out_refs = outs[1:]
        for n in range(2):
            index = prior_refs[2 * side + n][HD : HD + BLOCK // LANES, 0:LANES].astype(F32).astype(jnp.int32)
            index = jnp.concatenate([index[r : r + 1] for r in range(BLOCK // LANES)], axis=1)
            key_ref[n] = slot_rows(index, experts, capacity)
        second = ((place // 2) ^ side) == 1
        if early_sum is None:
            for n in range(lasts):
                outs[0][n] = jnp.zeros((width, width), F32)
            for i in range(half):
                arrive(i, True)

            @pl.loop(0, half)
            def _(i):
                rows_in = fixed[0][rows_of(i), :]
                for n, w_ref in enumerate(w_refs):
                    k = dot_nt(rows_in, w_ref[width : 2 * width, :]).astype(BF16)
                    v = dot_nt(rows_in, w_ref[2 * width : 3 * width, :]).astype(BF16)
                    outs[0][n] += jnp.where(same_heads, dot_tn(k, v), 0.0)

        early_ref = outs[0] if early_sum is None else refs[0]
        for n in range(lasts):
            state_ref[n] = states[count + n].astype(F32) + jnp.where(second, early_ref[n], 0.0)

        @pl.loop(0, half)
        def _(i):
            at = rows_of(i)
            relative = (place ^ i) % 2
            arrive(i)
            attended = [
                kept[2 * m + 1][at, 0:width].astype(F32) + dot_nn(kept[2 * m][at, 0:width], states[m])
                for m in range(count)
            ]
            for n, w_ref in enumerate(w_refs):
                _, last, state_ref[n] = attend_rows(normed_ref[at, :], w_ref, width, state_ref[n])
                attended.append(last)
            heads = []
            for values in attended:
                mean = dot_nn((values * values).astype(BF16), averaging)
                heads.append((values * lax.rsqrt(mean + EPS)).astype(BF16))
            total = tok_ref[at, :].astype(F32) + dot_nn(jnp.concatenate(heads, axis=1), proj_ref[...])
            stream = total.astype(BF16)
            moe_in = rms(stream.astype(F32)).astype(BF16)
            if side == 0:

                @pl.when(relative == 0)
                def _():
                    outs[0][...] = stream

            for local in range(EXP_DEV):
                picked = pick(key_ref[relative], moe_in, meta_ref[0], place, local, n_seq, n_ep, capacity)
                for k in range(n_seq):
                    out_refs[k // 2][k % 2, relative, local] = picked[k * capacity : (k + 1) * capacity]

    extra = ((lasts, width, width), F32) if early_sum is None else ((BLOCK, model), BF16)
    cells = model // CELL
    parts = [(TOKENS, cells), (NORMED, cells)] + [(HEADS + n, 1) for n in range(2 * count)]
    return call(
        kernel,
        [extra] + [((2, 2, EXP_DEV, capacity, model), BF16)] * (n_seq // 2),
        [meta, same, other, *priors, *projections] + ([] if early_sum is None else [early_sum]),
        13,
        [pltpu.VMEM((n_ep * width, model), BF16), pltpu.VMEM((lasts, width, width), F32)]
        + [pltpu.VMEM((2, 1, BLOCK), jnp.int32)]
        + [pltpu.VMEM((4 * width, model), BF16)] * lasts,
        space=space,
        reads=parts + ([(NORMED, cells)] if early_sum is None else []),
        steps=half,
        block=block,
        moving=len(parts),
    )


def expert(got, crossed, expert_in, expert_out, local, pairs=()):
    _, blocks, _, capacity, model = got[0].shape
    count = len(got)
    span = 2 * count * capacity

    def kernel(*refs):
        got_refs, (crossed_ref, w1, w2) = refs[:count], refs[count : count + 3]
        pair_refs, out_refs = refs[count + 3 : count + 3 + 2 * len(pairs)], refs[count + 3 + 2 * len(pairs) :]
        for n in range(len(pairs)):
            both = pair_refs[2 * n][...].astype(F32) + pair_refs[2 * n + 1][...].astype(F32)
            out_refs[blocks + n][...] = both.astype(BF16)
        pieces = []
        for n in range(blocks):
            for i in range(count):
                pieces += [got_refs[i][0, n, local], crossed_ref[i, n, local]]
        active = jnp.maximum(dot_nn(jnp.concatenate(pieces, axis=0), w1[local]), 0.0).astype(BF16)
        made = dot_nn(active, w2[local]).astype(BF16)
        for n in range(blocks):
            out_refs[n][...] = made[n * span : (n + 1) * span]

    flat = [a for pair in pairs for a in pair]
    out = pl.pallas_call(
        kernel,
        in_specs=[pl.BlockSpec(memory_space=pltpu.VMEM)] * (count + 3 + len(flat)),
        out_specs=[pl.BlockSpec(memory_space=pltpu.VMEM)] * (blocks + len(pairs)),
        out_shape=[jax.ShapeDtypeStruct((span, model), BF16)] * (blocks + len(pairs)),
        compiler_params=pltpu.CompilerParams(vmem_limit_bytes=EXPERT_VMEM_BYTES),
        cost_estimate=pl.CostEstimate(flops=int(3 * FLOPS), bytes_accessed=1 << 20, transcendentals=0),
    )(*got, crossed, expert_in, expert_out, *flat)
    return out[:blocks], out[blocks:]


def lay_out(meta, own, half, other, n_seq, capacity):
    model = own.shape[1]

    def kernel(ins, outs, scratch, arrive, leave, reads, writes):
        _, own_ref, half_ref, other_ref = ins
        both = (own_ref[...].astype(F32) + half_ref[...].astype(F32)).astype(BF16)
        for side, rows in enumerate((both, other_ref[...])):
            for k in range(n_seq):
                outs[k // 2][k % 2, side * capacity : (side + 1) * capacity, :] = rows[k * capacity : (k + 1) * capacity]

    return call(
        kernel, [((2, 2 * capacity, model), BF16)] * (n_seq // 2), [meta, own, half, other], 0.6
    )


def combine(meta, total, slots, returned, local, n_seq, n_ep, capacity, dtype):
    rows, model = total.shape
    got, crossed = returned

    def kernel(ins, outs, scratch, arrive, leave, reads, writes):
        meta_ref, total_ref, slot_ref, *got_refs, crossed_ref = ins
        span = 2 * capacity
        col = lax.broadcasted_iota(jnp.int32, (1, n_seq * span), 1)
        seq = (col // span) ^ meta_ref[0]
        pair = seq * (n_ep // 2) + ((col // capacity) % 2 ^ (meta_ref[1] // 2))
        key = (pair * EXP_DEV + local) * capacity + col % capacity
        hot = (slot_ref[...] == key).astype(BF16)
        pieces = []
        for i, got_ref in enumerate(got_refs):
            pieces += [got_ref[0], crossed_ref[i]]
        out = total_ref[...].astype(F32) + dot_nn(hot, jnp.concatenate(pieces, axis=0))
        outs[0][...] = out.astype(dtype)

    return call(kernel, [((rows, model), dtype)], [meta, total, slots, *got, crossed], 1.5)[0]


def per_device(tokens, input_proj, output_proj, expert_index, expert_in, expert_out):
    rows, model = tokens.shape
    width = output_proj.shape[0]
    n_seq, n_ep = lax.axis_size("seq"), lax.axis_size("ep")
    seq, ep = lax.axis_index("seq"), lax.axis_index("ep")
    meta = jnp.stack([seq, ep]).astype(jnp.int32)
    own_rows = rows // n_ep
    experts = EXP_DEV * n_seq * n_ep // 2
    capacity = max(2, 2 * own_rows // experts)

    def over_seq(x, bits):
        return lax.ppermute(x, "seq", xor_pairs(n_seq, bits)) if bits else x

    def over_ep(x, bits):
        return lax.ppermute(x, "ep", xor_pairs(n_ep, bits)) if bits else x

    def exchange(outgoing, after=()):
        got = [over_seq(out, 2 * i) for i, out in enumerate(outgoing)]
        got, after = lax.optimization_barrier((got, after))
        return got, over_seq(jnp.stack([g[1] for g in got]), 1)

    stacked = jnp.concatenate(
        [jnp.transpose(input_proj, (1, 2, 0)).reshape(3 * width, model), output_proj], axis=0
    )
    part = stacked.shape[0] // SPLIT
    along = [lax.dynamic_slice_in_dim(stacked, (seq % SPLIT) * part, part, 0)]
    for bit in range(n_ep.bit_length() - 1):
        along.append(over_ep(along[0], 1 << bit))

    own_sum, slots, space = attend_own(
        meta, tokens, stacked, expert_index, width, experts, capacity
    )
    along, own_sum = lax.optimization_barrier((along, own_sum))
    along = {0: along[0], **{1 << bit: a for bit, a in enumerate(along[1:])}}
    for m in range(1, n_ep):
        low = m & (m - 1)
        if low:
            along[m] = over_ep(along[low], m ^ low)

    def gather_layer(pieces):
        first = jnp.concatenate(pieces, axis=0)
        return [over_seq(first, bits) for bits in range(0, SPLIT, 2)]

    early = gather_layer([along[1], own_sum.reshape(-1, model)])
    later = [along[m] for m in range(2, n_ep)]
    later, early = lax.optimization_barrier((later, early))
    late = gather_layer(later)
    early = jnp.stack(early)
    early_other = over_seq(early, 1)

    sum_rows = own_sum.size // model
    sums = jnp.stack([early[:, -sum_rows:], early_other[:, -sum_rows:]], axis=1).reshape(SPLIT, HD, width)
    earlier = (jnp.arange(SPLIT) ^ (seq % SPLIT)) < seq % SPLIT
    prior = jnp.sum(jnp.where(earlier[:, None, None], sums.astype(F32), 0.0), axis=0)
    total, bit = jnp.sum(sums.astype(F32), axis=0), SPLIT
    while bit < n_seq:
        arrived = over_seq(total.astype(BF16), bit).astype(F32)
        prior = prior + jnp.where((seq & bit) != 0, arrived, 0.0)
        total, bit = total + arrived, 2 * bit
    index_rows = jnp.pad(
        expert_index.astype(BF16).reshape(own_rows // LANES, LANES), ((0, 4), (0, width - LANES))
    )
    prior = jnp.concatenate([prior.astype(BF16), index_rows], axis=0)
    priors = [prior]
    for m in range(1, n_ep):
        low = m & (m - 1)
        priors.append(over_ep(priors[low], m ^ low))

    early, prior = lax.optimization_barrier((early, prior))
    proj, space = attend_other(meta, space, early, early_other, 1, width, rows, model)
    projections = [output_proj, proj]
    late, projections, priors = lax.optimization_barrier((late, projections, priors))
    late = jnp.stack(late)
    late_other = over_seq(late, 1)
    def send(side, early_sum):
        return route(
            meta, space, late, late_other, projections, priors, side, early_sum, rows, n_seq, n_ep, capacity, experts
        )

    early_sum, *outgoing = send(1, None)
    stream, *outgoing_own = send(0, early_sum)
    got, crossed = exchange(outgoing, outgoing_own)
    outgoing_own, got = lax.optimization_barrier((outgoing_own, got))
    made, halves = [], []
    for local in range(EXP_DEV):
        if made:
            crossed, made = lax.optimization_barrier((crossed, made))
        made.append(expert(got, crossed, expert_in, expert_out, local)[0])
        halves.append(over_ep(made[-1][1], 1))
    got, crossed = exchange(outgoing_own, halves)
    owns, sides = [], []
    for local in range(EXP_DEV):
        if owns:
            crossed, owns = lax.optimization_barrier((crossed, owns))
        pair = (made[local][0], halves[local])
        own, sums = expert(got, crossed, expert_in, expert_out, local, [pair])
        owns.append(own)
        sides.append([own[0], over_ep(own[1], 1), over_ep(sums[0], 2)])
    sides[0], owns = lax.optimization_barrier((sides[0], owns))
    total, returned = stream, None
    for local in range(EXP_DEV):
        laid = lay_out(meta, *sides[local], n_seq, capacity)
        returned = exchange(laid, total if returned else sides[1:])
        last = local == EXP_DEV - 1
        total = combine(meta, total, slots, returned, local, n_seq, n_ep, capacity, BF16 if last else F32)
    return total


def solution(mesh):
    return jax.shard_map(
        per_device,
        mesh=mesh,
        in_specs=(
            P("seq", None),
            P(None, None, "ep"),
            P("ep", None),
            P(("seq", "ep"), None),
            P(("seq", "ep"), None, None),
            P(("seq", "ep"), None, None),
        ),
        out_specs=P(("seq", "ep"), None),
        check_vma=False,
    )
```

```python
import jax
import jax.numpy as jnp
from jax import lax
from jax.experimental import pallas as pl
from jax.experimental.pallas import tpu as pltpu
from jax.sharding import PartitionSpec as P

HD = 64
EXP_DEV = 2
BLOCK = 512
CHUNK = 256
SPLIT = 8
EPS = 1e-05
VMEM_BYTES = 40 * 1024 * 1024
EXPERT_VMEM_BYTES = 16 * 1024 * 1024
LANES = 128
FLOPS = 1.15e9
CELL = 256
CELLS = 26
NORMED, TOKENS, HEADS = 0, 3, 6

F32 = jnp.float32
BF16 = jnp.bfloat16


def xor_pairs(count, bits):
    return [(place, place ^ bits) for place in range(count)]


def dot_nt(a, b):
    return lax.dot_general(a, b, (((1,), (1,)), ((), ())), preferred_element_type=F32)


def dot_tn(a, b):
    return lax.dot_general(a, b, (((0,), (0,)), ((), ())), preferred_element_type=F32)


def dot_nn(a, b):
    return jnp.dot(a, b, preferred_element_type=F32)


def two_terms(x):
    high = x.astype(BF16)
    return high, (x - high.astype(F32)).astype(BF16)


def rms(values):
    return values * lax.rsqrt(jnp.mean(values * values, axis=-1, keepdims=True) + EPS)


def same_head(width):
    rows = lax.broadcasted_iota(jnp.int32, (width, width), 0) // HD
    cols = lax.broadcasted_iota(jnp.int32, (width, width), 1) // HD
    return rows == cols


def rows_of(i):
    return pl.ds(pl.multiple_of(i * BLOCK, BLOCK), BLOCK)


def call(kernel, out_shape, args, micros, scratch=(), space=None, reads=(), writes=(), steps=0, block=None, moving=None):
    given = [] if space is None else [space]
    rows = steps * BLOCK
    made = [] if not writes else [jax.ShapeDtypeStruct((CELLS, rows, CELL), BF16)]
    buffers = [pltpu.VMEM((rows, count * CELL), BF16) for _, count in (*reads, *writes)]
    sems = [pltpu.SemaphoreType.DMA((len(buffers), steps))] if buffers else []

    def body(*refs):
        ins, refs = refs[: len(args)], refs[len(args) :]
        given_ref, refs = refs[: len(given)], refs[len(given) :]
        outs, refs = refs[: len(out_shape)], refs[len(out_shape) :]
        made_ref, refs = refs[: len(made)], refs[len(made) :]
        own, held, sem = refs[: len(scratch)], refs[len(scratch) : len(scratch) + len(buffers)], refs[-1:]

        def copies(n, i):
            first, count = (*reads, *writes)[n]
            at = i if block is None or n >= moving else block(ins[0], i)
            there, here = rows_of(at), rows_of(i)
            for cell in range(count):
                near = held[n].at[here, pl.ds(cell * CELL, CELL)]
                if n < len(reads):
                    yield pltpu.make_async_copy(given_ref[0].at[first + cell, there], near, sem[0].at[n, i])
                else:
                    yield pltpu.make_async_copy(near, made_ref[0].at[first + cell, there], sem[0].at[n, i])

        split = len(reads) if moving is None else moving

        def fetch(i, parts):
            for n in parts:
                for copy in copies(n, i):
                    copy.start()

        def arrive(i, fixed=False):
            parts = range(split, len(reads)) if fixed else range(split)
            for n in parts:
                for copy in copies(n, i):
                    copy.wait()
            if not fixed:

                @pl.when(i + 1 < steps)
                def _():
                    fetch(i + 1, parts)

        def leave(i):
            for n in range(len(reads), len(buffers)):
                for copy in copies(n, i):
                    copy.start()

        if reads:
            for i in range(steps):
                fetch(i, range(split, len(reads)))
            fetch(0, range(split))
        kernel(ins, outs, own, arrive, leave, held[: len(reads)], held[len(reads) :])
        if writes:

            @pl.loop(0, steps)
            def _(i):
                for n in range(len(reads), len(buffers)):
                    for copy in copies(n, i):
                        copy.wait()

    return pl.pallas_call(
        body,
        in_specs=[pl.BlockSpec(memory_space=pltpu.SMEM)]
        + [pl.BlockSpec(memory_space=pltpu.VMEM)] * (len(args) - 1)
        + [pl.BlockSpec(memory_space=pl.ANY)] * len(given),
        out_specs=[pl.BlockSpec(memory_space=pltpu.VMEM)] * len(out_shape)
        + [pl.BlockSpec(memory_space=pl.ANY)] * len(made),
        out_shape=[jax.ShapeDtypeStruct(shape, dtype) for shape, dtype in out_shape] + made,
        scratch_shapes=[*scratch, *buffers, *sems],
        input_output_aliases={len(args): len(out_shape)} if given and made else {},
        compiler_params=pltpu.CompilerParams(vmem_limit_bytes=VMEM_BYTES),
        cost_estimate=pl.CostEstimate(flops=int(micros * FLOPS), bytes_accessed=1 << 20, transcendentals=0),
    )(*args, *given)


def attend_rows(normed, w_ref, width, state):
    q_all = dot_nt(normed, w_ref[0:width, :]).astype(BF16)
    k_all = dot_nt(normed, w_ref[width : 2 * width, :]).astype(BF16)
    v_all = dot_nt(normed, w_ref[2 * width : 3 * width, :]).astype(BF16)
    heads = width // HD
    head_of = lax.broadcasted_iota(jnp.int32, (CHUNK, width), 1) // HD
    causal = lax.broadcasted_iota(jnp.int32, (CHUNK, CHUNK), 0) >= lax.broadcasted_iota(
        jnp.int32, (CHUNK, CHUNK), 1
    )
    same = same_head(width)
    zero = jnp.zeros((), BF16)
    out = []
    for c in range(normed.shape[0] // CHUNK):
        q, k, v = (a[c * CHUNK : (c + 1) * CHUNK] for a in (q_all, k_all, v_all))
        attended = dot_nn(q, state.astype(BF16))
        stacked_q = jnp.concatenate([jnp.where(head_of == h, q, zero) for h in range(heads)], axis=0)
        scores = dot_nt(stacked_q, k)
        weights = jnp.concatenate(
            [jnp.where(causal, scores[h * CHUNK : (h + 1) * CHUNK], 0.0).astype(BF16) for h in range(heads)],
            axis=1,
        )
        stacked_v = jnp.concatenate([jnp.where(head_of == h, v, zero) for h in range(heads)], axis=0)
        out.append(attended + dot_nn(weights, stacked_v))
        state = state + jnp.where(same, dot_tn(k, v), 0.0)
    return q_all, jnp.concatenate(out, axis=0), state


def spread_heads(prior, width):
    spread = jnp.concatenate([prior] * (width // HD), axis=0)
    return jnp.where(same_head(width), spread, jnp.zeros((), prior.dtype))


def attend_own(meta, tokens, stacked, chosen, width, experts, capacity):
    rows, model = tokens.shape
    steps = rows // BLOCK

    def kernel(ins, outs, scratch, arrive, leave, reads, writes):
        _, w_ref, idx_ref, tok_ref = ins
        sum_ref, slot_ref = outs
        normed_ref, kept_ref, q_ref, att_ref = writes
        slot_ref[...] = slot_cols(idx_ref[...], experts, capacity)
        state = jnp.zeros((width, width), F32)
        for i in range(steps):
            at = slice(i * BLOCK, (i + 1) * BLOCK)
            kept_ref[at, :] = tok_ref[at, :]
            normed = rms(tok_ref[at, :].astype(F32)).astype(BF16)
            normed_ref[at, :] = normed
            q_ref[at, 0:width], attended, state = attend_rows(normed, w_ref, width, state)
            att_ref[at, 0:width] = attended.astype(BF16)
            leave(i)
        total = state[:HD]
        for head in range(1, width // HD):
            total = total + state[head * HD : (head + 1) * HD]
        sum_ref[...] = total.astype(BF16)

    cells = model // CELL
    return call(
        kernel,
        [((HD, width), BF16), (chosen.shape, jnp.int32)],
        [meta, stacked, chosen, tokens],
        7,
        writes=[(NORMED, cells), (TOKENS, cells), (HEADS, 1), (HEADS + 1, 1)],
        steps=steps,
    )


def place_slices(meta_ref, same_ref, other_ref, shard, w_ref):
    part = w_ref.shape[0] // SPLIT
    for parity, ref in enumerate((same_ref, other_ref)):
        for i in range(same_ref.shape[0]):
            place = (meta_ref[0] % SPLIT) ^ (2 * i + parity)
            at = pl.ds(pl.multiple_of(place * part, part), part)
            w_ref[at, :] = ref[i, shard * part : (shard + 1) * part]


def attend_other(meta, space, same, other, shard, width, rows, model):
    steps = rows // BLOCK

    def kernel(ins, outs, scratch, arrive, leave, reads, writes):
        meta_ref, same_ref, other_ref = ins
        (normed_ref,), (q_ref, att_ref), (w_ref, state_ref) = reads, writes, scratch
        place_slices(meta_ref, same_ref, other_ref, 0, w_ref)
        outs[0][...] = w_ref[3 * width : 4 * width, :]
        state_ref[...] = jnp.zeros((width, width), F32)

        @pl.loop(0, steps, unroll=2)
        def _(i):
            at = rows_of(i)
            arrive(i)
            q_ref[at, 0:width], attended, state_ref[...] = attend_rows(
                normed_ref[at, :], w_ref, width, state_ref[...]
            )
            att_ref[at, 0:width] = attended.astype(BF16)
            leave(i)

    first = HEADS + 2 * shard
    return call(
        kernel,
        [((width, model), BF16)],
        [meta, same, other],
        8,
        [pltpu.VMEM((4 * width, model), BF16), pltpu.VMEM((width, width), F32)],
        space=space,
        reads=[(NORMED, model // CELL)],
        writes=[(first, 1), (first + 1, 1)],
        steps=steps,
    )


def slot_rows(chosen, experts, capacity):
    rows = chosen.shape[1]
    hot = chosen == lax.broadcasted_iota(jnp.int32, (experts, rows), 0)
    before = lax.broadcasted_iota(jnp.int32, (rows, rows), 0) < lax.broadcasted_iota(
        jnp.int32, (rows, rows), 1
    )
    preceding = dot_nn(hot.astype(BF16), before.astype(BF16))
    rank = jnp.sum(jnp.where(hot, preceding, 0.0), axis=0, keepdims=True)
    return chosen * capacity + rank.astype(jnp.int32)


def slot_cols(chosen, experts, capacity):
    rows = chosen.shape[0]
    hot = chosen == lax.broadcasted_iota(jnp.int32, (rows, experts), 1)
    before = lax.broadcasted_iota(jnp.int32, (rows, rows), 0) > lax.broadcasted_iota(
        jnp.int32, (rows, rows), 1
    )
    preceding = dot_nn(before.astype(BF16), hot.astype(BF16))
    rank = jnp.sum(jnp.where(hot, preceding, 0.0), axis=1, keepdims=True)
    return chosen * capacity + rank.astype(jnp.int32)


def pick(slots_row, moe_in, seq, ep, local, n_seq, n_ep, capacity):
    wanted = n_seq * capacity
    row = lax.broadcasted_iota(jnp.int32, (wanted, 1), 0)
    pair = ((row // capacity) ^ seq) * (n_ep // 2) + ep // 2
    key = (pair * EXP_DEV + local) * capacity + row % capacity
    hot = (key == slots_row).astype(BF16)
    return dot_nn(hot, moe_in).astype(BF16)


def route(meta, space, same, other, projections, priors, side, early_sum, rows, n_seq, n_ep, capacity, experts):
    width, model = projections[0].shape
    count = len(projections)
    lasts = n_ep - count
    half = rows // BLOCK // 2

    def block(meta_ref, i):
        return half * ((meta_ref[1] // 2) ^ side) + i

    def kernel(ins, outs, scratch, arrive, leave, reads, writes):
        meta_ref, same_ref, other_ref, *refs = ins
        prior_refs, proj_refs, refs = refs[:n_ep], refs[n_ep : n_ep + count], refs[n_ep + count :]
        proj_ref, state_ref, key_ref, *w_refs = scratch
        (tok_ref, normed_ref, *kept), fixed = reads[: 2 + 2 * count], reads[2 + 2 * count :]
        for m in range(count):
            proj_ref[m * width : (m + 1) * width, :] = proj_refs[m][...]
        for n, w_ref in enumerate(w_refs):
            m = count + n
            place_slices(meta_ref, same_ref, other_ref, n, w_ref)
            proj_ref[m * width : (m + 1) * width, :] = w_ref[3 * width : 4 * width, :]
        same_heads = same_head(width)
        states = [spread_heads(ref[0:HD, :], width) for ref in prior_refs]
        averaging = jnp.where(same_heads, 1.0 / HD, 0.0).astype(BF16)
        place = meta_ref[1]
        out_refs = outs[1:]
        for n in range(2):
            index = prior_refs[2 * side + n][HD : HD + BLOCK // LANES, 0:LANES].astype(F32).astype(jnp.int32)
            index = jnp.concatenate([index[r : r + 1] for r in range(BLOCK // LANES)], axis=1)
            key_ref[n] = slot_rows(index, experts, capacity)
        second = ((place // 2) ^ side) == 1
        if early_sum is None:
            for n in range(lasts):
                outs[0][n] = jnp.zeros((width, width), F32)
            for i in range(half):
                arrive(i, True)

            @pl.loop(0, half)
            def _(i):
                rows_in = fixed[0][rows_of(i), :]
                for n, w_ref in enumerate(w_refs):
                    k = dot_nt(rows_in, w_ref[width : 2 * width, :]).astype(BF16)
                    v = dot_nt(rows_in, w_ref[2 * width : 3 * width, :]).astype(BF16)
                    outs[0][n] += jnp.where(same_heads, dot_tn(k, v), 0.0)

        early_ref = outs[0] if early_sum is None else refs[0]
        for n in range(lasts):
            state_ref[n] = states[count + n].astype(F32) + jnp.where(second, early_ref[n], 0.0)

        @pl.loop(0, half)
        def _(i):
            at = rows_of(i)
            relative = (place ^ i) % 2
            arrive(i)
            attended = [
                kept[2 * m + 1][at, 0:width].astype(F32) + dot_nn(kept[2 * m][at, 0:width], states[m])
                for m in range(count)
            ]
            for n, w_ref in enumerate(w_refs):
                _, last, state_ref[n] = attend_rows(normed_ref[at, :], w_ref, width, state_ref[n])
                attended.append(last)
            heads = []
            for values in attended:
                mean = dot_nn((values * values).astype(BF16), averaging)
                heads.append((values * lax.rsqrt(mean + EPS)).astype(BF16))
            total = tok_ref[at, :].astype(F32) + dot_nn(jnp.concatenate(heads, axis=1), proj_ref[...])
            stream = total.astype(BF16)
            moe_in = rms(stream.astype(F32)).astype(BF16)
            if side == 0:

                @pl.when(relative == 0)
                def _():
                    outs[0][...] = stream

            for local in range(EXP_DEV):
                picked = pick(key_ref[relative], moe_in, meta_ref[0], place, local, n_seq, n_ep, capacity)
                for k in range(n_seq):
                    out_refs[k // 2][k % 2, relative, local] = picked[k * capacity : (k + 1) * capacity]

    extra = ((lasts, width, width), F32) if early_sum is None else ((BLOCK, model), BF16)
    cells = model // CELL
    parts = [(TOKENS, cells), (NORMED, cells)] + [(HEADS + n, 1) for n in range(2 * count)]
    return call(
        kernel,
        [extra] + [((2, 2, EXP_DEV, capacity, model), BF16)] * (n_seq // 2),
        [meta, same, other, *priors, *projections] + ([] if early_sum is None else [early_sum]),
        13,
        [pltpu.VMEM((n_ep * width, model), BF16), pltpu.VMEM((lasts, width, width), F32)]
        + [pltpu.VMEM((2, 1, BLOCK), jnp.int32)]
        + [pltpu.VMEM((4 * width, model), BF16)] * lasts,
        space=space,
        reads=parts + ([(NORMED, cells)] if early_sum is None else []),
        steps=half,
        block=block,
        moving=len(parts),
    )


def expert(got, crossed, expert_in, expert_out, local, pairs=()):
    _, blocks, _, capacity, model = got[0].shape
    count = len(got)
    span = 2 * count * capacity
    flat = [a for pair in pairs for a in pair]

    def kernel(*refs):
        got_refs, (crossed_ref, w1, w2) = refs[:count], refs[count : count + 3]
        pair_refs, out_refs = list(refs[count + 3 : count + 3 + len(flat)]), refs[count + 3 + len(flat) :]
        for n, (kept, *pieces) in enumerate(pairs):
            kept_ref, first = pair_refs.pop(0), 0
            for piece in pieces:
                at = slice(first, first + piece.shape[0])
                both = kept_ref[at, :].astype(F32) + pair_refs.pop(0)[...].astype(F32)
                out_refs[blocks + n][at, :] = both.astype(BF16)
                first += piece.shape[0]
        pieces = []
        for n in range(blocks):
            for i in range(count):
                pieces += [got_refs[i][0, n, local], crossed_ref[i, n, local]]
        active = jnp.maximum(dot_nn(jnp.concatenate(pieces, axis=0), w1[local]), 0.0).astype(BF16)
        made = dot_nn(active, w2[local]).astype(BF16)
        for n in range(blocks):
            out_refs[n][...] = made[n * span : (n + 1) * span]

    out = pl.pallas_call(
        kernel,
        in_specs=[pl.BlockSpec(memory_space=pltpu.VMEM)] * (count + 3 + len(flat)),
        out_specs=[pl.BlockSpec(memory_space=pltpu.VMEM)] * (blocks + len(pairs)),
        out_shape=[jax.ShapeDtypeStruct((span, model), BF16)] * (blocks + len(pairs)),
        compiler_params=pltpu.CompilerParams(vmem_limit_bytes=EXPERT_VMEM_BYTES),
        cost_estimate=pl.CostEstimate(flops=int(3 * FLOPS), bytes_accessed=1 << 20, transcendentals=0),
    )(*got, crossed, expert_in, expert_out, *flat)
    return out[:blocks], out[blocks:]


def lay_out(meta, own, half, other, n_seq, capacity):
    model = own.shape[1]

    def kernel(ins, outs, scratch, arrive, leave, reads, writes):
        _, own_ref, half_ref, other_ref = ins
        both = (own_ref[...].astype(F32) + half_ref[...].astype(F32)).astype(BF16)
        for side, rows in enumerate((both, other_ref[...])):
            for k in range(n_seq):
                outs[k // 2][k % 2, side * capacity : (side + 1) * capacity, :] = rows[k * capacity : (k + 1) * capacity]

    return call(
        kernel, [((2, 2 * capacity, model), BF16)] * (n_seq // 2), [meta, own, half, other], 0.6
    )


def combine(meta, total, slots, returned, local, n_seq, n_ep, capacity, dtype):
    rows, model = total.shape
    got, crossed = returned

    def kernel(ins, outs, scratch, arrive, leave, reads, writes):
        meta_ref, total_ref, slot_ref, *got_refs, crossed_ref = ins
        span = 2 * capacity
        col = lax.broadcasted_iota(jnp.int32, (1, n_seq * span), 1)
        seq = (col // span) ^ meta_ref[0]
        pair = seq * (n_ep // 2) + ((col // capacity) % 2 ^ (meta_ref[1] // 2))
        key = (pair * EXP_DEV + local) * capacity + col % capacity
        hot = (slot_ref[...] == key).astype(BF16)
        pieces = []
        for i, got_ref in enumerate(got_refs):
            pieces += [got_ref[0], crossed_ref[i]]
        out = total_ref[...].astype(F32) + dot_nn(hot, jnp.concatenate(pieces, axis=0))
        outs[0][...] = out.astype(dtype)

    return call(kernel, [((rows, model), dtype)], [meta, total, slots, *got, crossed], 1.5)[0]


def per_device(tokens, input_proj, output_proj, expert_index, expert_in, expert_out):
    rows, model = tokens.shape
    width = output_proj.shape[0]
    n_seq, n_ep = lax.axis_size("seq"), lax.axis_size("ep")
    seq, ep = lax.axis_index("seq"), lax.axis_index("ep")
    meta = jnp.stack([seq, ep]).astype(jnp.int32)
    own_rows = rows // n_ep
    experts = EXP_DEV * n_seq * n_ep // 2
    capacity = max(2, 2 * own_rows // experts)

    def over_seq(x, bits):
        return lax.ppermute(x, "seq", xor_pairs(n_seq, bits)) if bits else x

    def over_ep(x, bits):
        return lax.ppermute(x, "ep", xor_pairs(n_ep, bits)) if bits else x

    def exchange(outgoing, after=()):
        got = [over_seq(out, 2 * i) for i, out in reversed(list(enumerate(outgoing)))][::-1]
        got, after = lax.optimization_barrier((got, after))
        return got, over_seq(jnp.stack([g[1] for g in got]), 1)

    stacked = jnp.concatenate(
        [jnp.transpose(input_proj, (1, 2, 0)).reshape(3 * width, model), output_proj], axis=0
    )
    part = stacked.shape[0] // SPLIT
    along = [lax.dynamic_slice_in_dim(stacked, (seq % SPLIT) * part, part, 0)]
    for bit in range(n_ep.bit_length() - 1):
        along.append(over_ep(along[0], 1 << bit))

    own_sum, slots, space = attend_own(
        meta, tokens, stacked, expert_index, width, experts, capacity
    )
    along, own_sum = lax.optimization_barrier((along, own_sum))
    along = {0: along[0], **{1 << bit: a for bit, a in enumerate(along[1:])}}
    for m in range(1, n_ep):
        low = m & (m - 1)
        if low:
            along[m] = over_ep(along[low], m ^ low)

    def gather_layer(pieces):
        first = jnp.concatenate(pieces, axis=0)
        return [over_seq(first, bits) for bits in reversed(range(0, SPLIT, 2))][::-1]

    early = gather_layer([along[1], own_sum.reshape(-1, model)])
    later = [along[m] for m in range(2, n_ep)]
    later, early = lax.optimization_barrier((later, early))
    late = gather_layer(later)
    early = jnp.stack(early)
    early_other = over_seq(early, 1)

    sum_rows = own_sum.size // model
    sums = jnp.stack([early[:, -sum_rows:], early_other[:, -sum_rows:]], axis=1).reshape(SPLIT, HD, width)
    earlier = (jnp.arange(SPLIT) ^ (seq % SPLIT)) < seq % SPLIT
    prior = jnp.sum(jnp.where(earlier[:, None, None], sums.astype(F32), 0.0), axis=0)
    total, bit = jnp.sum(sums.astype(F32), axis=0), SPLIT
    while bit < n_seq:
        arrived = over_seq(total.astype(BF16), bit).astype(F32)
        prior = prior + jnp.where((seq & bit) != 0, arrived, 0.0)
        total, bit = total + arrived, 2 * bit
    index_rows = jnp.pad(
        expert_index.astype(BF16).reshape(own_rows // LANES, LANES), ((0, 4), (0, width - LANES))
    )
    prior = jnp.concatenate([prior.astype(BF16), index_rows], axis=0)
    priors = [prior]
    for m in range(1, n_ep):
        low = m & (m - 1)
        priors.append(over_ep(priors[low], m ^ low))

    early, prior = lax.optimization_barrier((early, prior))
    proj, space = attend_other(meta, space, early, early_other, 1, width, rows, model)
    projections = [output_proj, proj]
    late, projections, priors = lax.optimization_barrier((late, projections, priors))
    late = jnp.stack(late)
    late_other = over_seq(late, 1)
    def send(side, early_sum):
        return route(
            meta, space, late, late_other, projections, priors, side, early_sum, rows, n_seq, n_ep, capacity, experts
        )

    early_sum, *outgoing = send(1, None)
    stream, *outgoing_own = send(0, early_sum)
    got, crossed = exchange(outgoing, outgoing_own)
    outgoing_own, got = lax.optimization_barrier((outgoing_own, got))
    made, halves = [], []
    for local in range(EXP_DEV):
        if made:
            crossed, made = lax.optimization_barrier((crossed, made))
        made.append(expert(got, crossed, expert_in, expert_out, local)[0])
        cuts = jnp.split(made[-1][1], 1 + (local > 0))
        halves.append([over_ep(piece, 1) for piece in cuts])
    got, crossed = exchange(outgoing_own, ([half[0] for half in halves], made))
    owns, sides = [], []
    for local in range(EXP_DEV):
        if owns:
            crossed, owns = lax.optimization_barrier((crossed, owns))
        pair = (made[local][0], *halves[local])
        own, sums = expert(got, crossed, expert_in, expert_out, local, [pair])
        owns.append(own)
        sides.append([own[0], over_ep(own[1], 1), over_ep(sums[0], 2)])
    sides[0], owns = lax.optimization_barrier((sides[0], owns))
    total, returned = stream, None
    for local in range(EXP_DEV):
        laid = lay_out(meta, *sides[local], n_seq, capacity)
        returned = exchange(laid, total if returned else sides[1:])
        last = local == EXP_DEV - 1
        total = combine(meta, total, slots, returned, local, n_seq, n_ep, capacity, BF16 if last else F32)
    return total


def solution(mesh):
    return jax.shard_map(
        per_device,
        mesh=mesh,
        in_specs=(
            P("seq", None),
            P(None, None, "ep"),
            P("ep", None),
            P(("seq", "ep"), None),
            P(("seq", "ep"), None, None),
            P(("seq", "ep"), None, None),
        ),
        out_specs=P(("seq", "ep"), None),
        check_vma=False,
    )
```

```python
import jax
import jax.numpy as jnp
from jax import lax
from jax.experimental import pallas as pl
from jax.experimental.pallas import tpu as pltpu
from jax.sharding import PartitionSpec as P

HD = 64
EXP_DEV = 2
BLOCK = 512
CHUNK = 256
SPLIT = 8
EPS = 1e-05
VMEM_BYTES = 40 * 1024 * 1024
EXPERT_VMEM_BYTES = 16 * 1024 * 1024
LANES = 128
FLOPS = 1.15e9
CELL = 256
CELLS = 26
NORMED, TOKENS, HEADS = 0, 3, 6

F32 = jnp.float32
BF16 = jnp.bfloat16


def xor_pairs(count, bits):
    return [(place, place ^ bits) for place in range(count)]


def dot_nt(a, b):
    return lax.dot_general(a, b, (((1,), (1,)), ((), ())), preferred_element_type=F32)


def dot_tn(a, b):
    return lax.dot_general(a, b, (((0,), (0,)), ((), ())), preferred_element_type=F32)


def dot_nn(a, b):
    return jnp.dot(a, b, preferred_element_type=F32)


def two_terms(x):
    high = x.astype(BF16)
    return high, (x - high.astype(F32)).astype(BF16)


def rms(values):
    return values * lax.rsqrt(jnp.mean(values * values, axis=-1, keepdims=True) + EPS)


def same_head(width):
    rows = lax.broadcasted_iota(jnp.int32, (width, width), 0) // HD
    cols = lax.broadcasted_iota(jnp.int32, (width, width), 1) // HD
    return rows == cols


def rows_of(i):
    return pl.ds(pl.multiple_of(i * BLOCK, BLOCK), BLOCK)


def call(kernel, out_shape, args, micros, scratch=(), space=None, reads=(), writes=(), steps=0, block=None, moving=None):
    given = [] if space is None else [space]
    rows = steps * BLOCK
    made = [] if not writes else [jax.ShapeDtypeStruct((CELLS, rows, CELL), BF16)]
    buffers = [pltpu.VMEM((rows, count * CELL), BF16) for _, count in (*reads, *writes)]
    sems = [pltpu.SemaphoreType.DMA((len(buffers), steps))] if buffers else []

    def body(*refs):
        ins, refs = refs[: len(args)], refs[len(args) :]
        given_ref, refs = refs[: len(given)], refs[len(given) :]
        outs, refs = refs[: len(out_shape)], refs[len(out_shape) :]
        made_ref, refs = refs[: len(made)], refs[len(made) :]
        own, held, sem = refs[: len(scratch)], refs[len(scratch) : len(scratch) + len(buffers)], refs[-1:]

        def copies(n, i):
            first, count = (*reads, *writes)[n]
            at = i if block is None or n >= moving else block(ins[0], i)
            there, here = rows_of(at), rows_of(i)
            for cell in range(count):
                near = held[n].at[here, pl.ds(cell * CELL, CELL)]
                if n < len(reads):
                    yield pltpu.make_async_copy(given_ref[0].at[first + cell, there], near, sem[0].at[n, i])
                else:
                    yield pltpu.make_async_copy(near, made_ref[0].at[first + cell, there], sem[0].at[n, i])

        split = len(reads) if moving is None else moving

        def fetch(i, parts):
            for n in parts:
                for copy in copies(n, i):
                    copy.start()

        def arrive(i, fixed=False):
            parts = range(split, len(reads)) if fixed else range(split)
            for n in parts:
                for copy in copies(n, i):
                    copy.wait()
            if not fixed:

                @pl.when(i + 1 < steps)
                def _():
                    fetch(i + 1, parts)

        def leave(i):
            for n in range(len(reads), len(buffers)):
                for copy in copies(n, i):
                    copy.start()

        if reads:
            for i in range(steps):
                fetch(i, range(split, len(reads)))
            fetch(0, range(split))
        kernel(ins, outs, own, arrive, leave, held[: len(reads)], held[len(reads) :])
        if writes:

            @pl.loop(0, steps)
            def _(i):
                for n in range(len(reads), len(buffers)):
                    for copy in copies(n, i):
                        copy.wait()

    return pl.pallas_call(
        body,
        in_specs=[pl.BlockSpec(memory_space=pltpu.SMEM)]
        + [pl.BlockSpec(memory_space=pltpu.VMEM)] * (len(args) - 1)
        + [pl.BlockSpec(memory_space=pl.ANY)] * len(given),
        out_specs=[pl.BlockSpec(memory_space=pltpu.VMEM)] * len(out_shape)
        + [pl.BlockSpec(memory_space=pl.ANY)] * len(made),
        out_shape=[jax.ShapeDtypeStruct(shape, dtype) for shape, dtype in out_shape] + made,
        scratch_shapes=[*scratch, *buffers, *sems],
        input_output_aliases={len(args): len(out_shape)} if given and made else {},
        compiler_params=pltpu.CompilerParams(vmem_limit_bytes=VMEM_BYTES),
        cost_estimate=pl.CostEstimate(flops=int(micros * FLOPS), bytes_accessed=1 << 20, transcendentals=0),
    )(*args, *given)


def attend_rows(normed, w_ref, width, state):
    q_all = dot_nt(normed, w_ref[0:width, :]).astype(BF16)
    k_all = dot_nt(normed, w_ref[width : 2 * width, :]).astype(BF16)
    v_all = dot_nt(normed, w_ref[2 * width : 3 * width, :]).astype(BF16)
    heads = width // HD
    head_of = lax.broadcasted_iota(jnp.int32, (CHUNK, width), 1) // HD
    causal = lax.broadcasted_iota(jnp.int32, (CHUNK, CHUNK), 0) >= lax.broadcasted_iota(
        jnp.int32, (CHUNK, CHUNK), 1
    )
    same = same_head(width)
    zero = jnp.zeros((), BF16)
    out = []
    for c in range(normed.shape[0] // CHUNK):
        q, k, v = (a[c * CHUNK : (c + 1) * CHUNK] for a in (q_all, k_all, v_all))
        attended = dot_nn(q, state.astype(BF16))
        stacked_q = jnp.concatenate([jnp.where(head_of == h, q, zero) for h in range(heads)], axis=0)
        scores = dot_nt(stacked_q, k)
        weights = jnp.concatenate(
            [jnp.where(causal, scores[h * CHUNK : (h + 1) * CHUNK], 0.0).astype(BF16) for h in range(heads)],
            axis=1,
        )
        stacked_v = jnp.concatenate([jnp.where(head_of == h, v, zero) for h in range(heads)], axis=0)
        out.append(attended + dot_nn(weights, stacked_v))
        state = state + jnp.where(same, dot_tn(k, v), 0.0)
    return q_all, jnp.concatenate(out, axis=0), state


def spread_heads(prior, width):
    spread = jnp.concatenate([prior] * (width // HD), axis=0)
    return jnp.where(same_head(width), spread, jnp.zeros((), prior.dtype))


def attend_own(meta, tokens, stacked, chosen, width, experts, capacity):
    rows, model = tokens.shape
    steps = rows // BLOCK

    def kernel(ins, outs, scratch, arrive, leave, reads, writes):
        _, w_ref, idx_ref, tok_ref = ins
        sum_ref, slot_ref = outs
        normed_ref, kept_ref, q_ref, att_ref = writes
        slot_ref[...] = slot_cols(idx_ref[...], experts, capacity)
        state = jnp.zeros((width, width), F32)
        for i in range(steps):
            at = slice(i * BLOCK, (i + 1) * BLOCK)
            kept_ref[at, :] = tok_ref[at, :]
            normed = rms(tok_ref[at, :].astype(F32)).astype(BF16)
            normed_ref[at, :] = normed
            q_ref[at, 0:width], attended, state = attend_rows(normed, w_ref, width, state)
            att_ref[at, 0:width] = attended.astype(BF16)
            leave(i)
        total = state[:HD]
        for head in range(1, width // HD):
            total = total + state[head * HD : (head + 1) * HD]
        sum_ref[...] = total.astype(BF16)

    cells = model // CELL
    return call(
        kernel,
        [((HD, width), BF16), (chosen.shape, jnp.int32)],
        [meta, stacked, chosen, tokens],
        7,
        writes=[(NORMED, cells), (TOKENS, cells), (HEADS, 1), (HEADS + 1, 1)],
        steps=steps,
    )


def place_slices(meta_ref, same_ref, other_ref, shard, w_ref):
    part = w_ref.shape[0] // SPLIT
    for parity, ref in enumerate((same_ref, other_ref)):
        for i in range(same_ref.shape[0]):
            place = (meta_ref[0] % SPLIT) ^ (2 * i + parity)
            at = pl.ds(pl.multiple_of(place * part, part), part)
            w_ref[at, :] = ref[i, shard * part : (shard + 1) * part]


def attend_other(meta, space, same, other, shard, width, rows, model):
    steps = rows // BLOCK

    def kernel(ins, outs, scratch, arrive, leave, reads, writes):
        meta_ref, same_ref, other_ref = ins
        (normed_ref,), (q_ref, att_ref), (w_ref, state_ref) = reads, writes, scratch
        place_slices(meta_ref, same_ref, other_ref, 0, w_ref)
        outs[0][...] = w_ref[3 * width : 4 * width, :]
        state_ref[...] = jnp.zeros((width, width), F32)

        @pl.loop(0, steps, unroll=2)
        def _(i):
            at = rows_of(i)
            arrive(i)
            q_ref[at, 0:width], attended, state_ref[...] = attend_rows(
                normed_ref[at, :], w_ref, width, state_ref[...]
            )
            att_ref[at, 0:width] = attended.astype(BF16)
            leave(i)

    first = HEADS + 2 * shard
    return call(
        kernel,
        [((width, model), BF16)],
        [meta, same, other],
        8,
        [pltpu.VMEM((4 * width, model), BF16), pltpu.VMEM((width, width), F32)],
        space=space,
        reads=[(NORMED, model // CELL)],
        writes=[(first, 1), (first + 1, 1)],
        steps=steps,
    )


def slot_rows(chosen, experts, capacity):
    rows = chosen.shape[1]
    hot = chosen == lax.broadcasted_iota(jnp.int32, (experts, rows), 0)
    before = lax.broadcasted_iota(jnp.int32, (rows, rows), 0) < lax.broadcasted_iota(
        jnp.int32, (rows, rows), 1
    )
    preceding = dot_nn(hot.astype(BF16), before.astype(BF16))
    rank = jnp.sum(jnp.where(hot, preceding, 0.0), axis=0, keepdims=True)
    return chosen * capacity + rank.astype(jnp.int32)


def slot_cols(chosen, experts, capacity):
    rows = chosen.shape[0]
    hot = chosen == lax.broadcasted_iota(jnp.int32, (rows, experts), 1)
    before = lax.broadcasted_iota(jnp.int32, (rows, rows), 0) > lax.broadcasted_iota(
        jnp.int32, (rows, rows), 1
    )
    preceding = dot_nn(before.astype(BF16), hot.astype(BF16))
    rank = jnp.sum(jnp.where(hot, preceding, 0.0), axis=1, keepdims=True)
    return chosen * capacity + rank.astype(jnp.int32)


def pick(slots_row, moe_in, seq, ep, local, n_seq, n_ep, capacity):
    wanted = n_seq * capacity
    row = lax.broadcasted_iota(jnp.int32, (wanted, 1), 0)
    pair = ((row // capacity) ^ seq) * (n_ep // 2) + ep // 2
    key = (pair * EXP_DEV + local) * capacity + row % capacity
    hot = (key == slots_row).astype(BF16)
    return dot_nn(hot, moe_in).astype(BF16)


def route(meta, space, same, other, projections, priors, side, early_sum, rows, n_seq, n_ep, capacity, experts):
    width, model = projections[0].shape
    count = len(projections)
    lasts = n_ep - count
    half = rows // BLOCK // 2

    def block(meta_ref, i):
        return half * ((meta_ref[1] // 2) ^ side) + i

    def kernel(ins, outs, scratch, arrive, leave, reads, writes):
        meta_ref, same_ref, other_ref, *refs = ins
        prior_refs, proj_refs, refs = refs[:n_ep], refs[n_ep : n_ep + count], refs[n_ep + count :]
        proj_ref, state_ref, key_ref, *w_refs = scratch
        (tok_ref, normed_ref, *kept), fixed = reads[: 2 + 2 * count], reads[2 + 2 * count :]
        for m in range(count):
            proj_ref[m * width : (m + 1) * width, :] = proj_refs[m][...]
        for n, w_ref in enumerate(w_refs):
            m = count + n
            place_slices(meta_ref, same_ref, other_ref, n, w_ref)
            proj_ref[m * width : (m + 1) * width, :] = w_ref[3 * width : 4 * width, :]
        same_heads = same_head(width)
        states = [spread_heads(ref[0:HD, :], width) for ref in prior_refs]
        averaging = jnp.where(same_heads, 1.0 / HD, 0.0).astype(BF16)
        place = meta_ref[1]
        out_refs = outs[1:]
        for n in range(2):
            index = prior_refs[2 * side + n][HD : HD + BLOCK // LANES, 0:LANES].astype(F32).astype(jnp.int32)
            index = jnp.concatenate([index[r : r + 1] for r in range(BLOCK // LANES)], axis=1)
            key_ref[n] = slot_rows(index, experts, capacity)
        second = ((place // 2) ^ side) == 1
        if early_sum is None:
            for n in range(lasts):
                outs[0][n] = jnp.zeros((width, width), F32)
            for i in range(half):
                arrive(i, True)

            @pl.loop(0, half)
            def _(i):
                rows_in = fixed[0][rows_of(i), :]
                for n, w_ref in enumerate(w_refs):
                    k = dot_nt(rows_in, w_ref[width : 2 * width, :]).astype(BF16)
                    v = dot_nt(rows_in, w_ref[2 * width : 3 * width, :]).astype(BF16)
                    outs[0][n] += jnp.where(same_heads, dot_tn(k, v), 0.0)

        early_ref = outs[0] if early_sum is None else refs[0]
        for n in range(lasts):
            state_ref[n] = states[count + n].astype(F32) + jnp.where(second, early_ref[n], 0.0)

        @pl.loop(0, half)
        def _(i):
            at = rows_of(i)
            relative = (place ^ i) % 2
            arrive(i)
            attended = [
                kept[2 * m + 1][at, 0:width].astype(F32) + dot_nn(kept[2 * m][at, 0:width], states[m])
                for m in range(count)
            ]
            for n, w_ref in enumerate(w_refs):
                _, last, state_ref[n] = attend_rows(normed_ref[at, :], w_ref, width, state_ref[n])
                attended.append(last)
            heads = []
            for values in attended:
                mean = dot_nn((values * values).astype(BF16), averaging)
                heads.append((values * lax.rsqrt(mean + EPS)).astype(BF16))
            total = tok_ref[at, :].astype(F32) + dot_nn(jnp.concatenate(heads, axis=1), proj_ref[...])
            stream = total.astype(BF16)
            moe_in = rms(stream.astype(F32)).astype(BF16)
            if side == 0:

                @pl.when(relative == 0)
                def _():
                    outs[0][...] = stream

            for local in range(EXP_DEV):
                picked = pick(key_ref[relative], moe_in, meta_ref[0], place, local, n_seq, n_ep, capacity)
                for k in range(n_seq):
                    out_refs[k // 2][k % 2, relative, local] = picked[k * capacity : (k + 1) * capacity]

    extra = ((lasts, width, width), F32) if early_sum is None else ((BLOCK, model), BF16)
    cells = model // CELL
    parts = [(TOKENS, cells), (NORMED, cells)] + [(HEADS + n, 1) for n in range(2 * count)]
    return call(
        kernel,
        [extra] + [((2, 2, EXP_DEV, capacity, model), BF16)] * (n_seq // 2),
        [meta, same, other, *priors, *projections] + ([] if early_sum is None else [early_sum]),
        13,
        [pltpu.VMEM((n_ep * width, model), BF16), pltpu.VMEM((lasts, width, width), F32)]
        + [pltpu.VMEM((2, 1, BLOCK), jnp.int32)]
        + [pltpu.VMEM((4 * width, model), BF16)] * lasts,
        space=space,
        reads=parts + ([(NORMED, cells)] if early_sum is None else []),
        steps=half,
        block=block,
        moving=len(parts),
    )


def expert(got, crossed, expert_in, expert_out, local, pairs=()):
    _, blocks, _, capacity, model = got[0].shape
    count = len(got)
    span = 2 * count * capacity
    flat = [a for pair in pairs for a in pair]

    def kernel(*refs):
        got_refs, (crossed_ref, w1, w2) = refs[:count], refs[count : count + 3]
        pair_refs, out_refs = list(refs[count + 3 : count + 3 + len(flat)]), refs[count + 3 + len(flat) :]
        for n, (kept, *pieces) in enumerate(pairs):
            kept_ref, first = pair_refs.pop(0), 0
            for piece in pieces:
                at = slice(first, first + piece.shape[0])
                both = kept_ref[at, :].astype(F32) + pair_refs.pop(0)[...].astype(F32)
                out_refs[blocks + n][at, :] = both.astype(BF16)
                first += piece.shape[0]
        pieces = []
        for n in range(blocks):
            for i in range(count):
                pieces += [got_refs[i][0, n, local], crossed_ref[i, n, local]]
        active = jnp.maximum(dot_nn(jnp.concatenate(pieces, axis=0), w1[local]), 0.0).astype(BF16)
        made = dot_nn(active, w2[local]).astype(BF16)
        for n in range(blocks):
            out_refs[n][...] = made[n * span : (n + 1) * span]

    out = pl.pallas_call(
        kernel,
        in_specs=[pl.BlockSpec(memory_space=pltpu.VMEM)] * (count + 3 + len(flat)),
        out_specs=[pl.BlockSpec(memory_space=pltpu.VMEM)] * (blocks + len(pairs)),
        out_shape=[jax.ShapeDtypeStruct((span, model), BF16)] * (blocks + len(pairs)),
        compiler_params=pltpu.CompilerParams(vmem_limit_bytes=EXPERT_VMEM_BYTES),
        cost_estimate=pl.CostEstimate(flops=int(3 * FLOPS), bytes_accessed=1 << 20, transcendentals=0),
    )(*got, crossed, expert_in, expert_out, *flat)
    return out[:blocks], out[blocks:]


def lay_out(meta, own, half, other, n_seq, capacity):
    model = own.shape[1]

    def kernel(ins, outs, scratch, arrive, leave, reads, writes):
        _, own_ref, half_ref, other_ref = ins
        both = (own_ref[...].astype(F32) + half_ref[...].astype(F32)).astype(BF16)
        for side, rows in enumerate((both, other_ref[...])):
            for k in range(n_seq):
                outs[k // 2][k % 2, side * capacity : (side + 1) * capacity, :] = rows[k * capacity : (k + 1) * capacity]

    return call(
        kernel, [((2, 2 * capacity, model), BF16)] * (n_seq // 2), [meta, own, half, other], 0.6
    )


def combine(meta, total, slots, returned, hots, n_seq, n_ep, capacity, dtype):
    rows, model = total.shape
    got, crossed = returned
    span = 2 * capacity

    def kernel(ins, outs, scratch, arrive, leave, reads, writes):
        meta_ref, total_ref, slot_ref, *got_refs, crossed_ref = ins
        if hots is None:
            col = lax.broadcasted_iota(jnp.int32, (1, n_seq * span), 1)
            seq = (col // span) ^ meta_ref[0]
            pair = seq * (n_ep // 2) + ((col // capacity) % 2 ^ (meta_ref[1] // 2))
            found = []
            for local in range(EXP_DEV):
                key = (pair * EXP_DEV + local) * capacity + col % capacity
                found.append((slot_ref[...] == key).astype(BF16))
            hot = found[0]
            for out, other in zip(outs[1:], found[1:]):
                out[...] = other
        else:
            hot = slot_ref[...]
        pieces = []
        for i, got_ref in enumerate(got_refs):
            pieces += [got_ref[0], crossed_ref[i]]
        out = total_ref[...].astype(F32) + dot_nn(hot, jnp.concatenate(pieces, axis=0))
        outs[0][...] = out.astype(dtype)

    others = [((rows, n_seq * span), BF16)] * (EXP_DEV - 1) if hots is None else []
    where = slots if hots is None else hots
    return call(kernel, [((rows, model), dtype)] + others, [meta, total, where, *got, crossed], 1.5)


def per_device(tokens, input_proj, output_proj, expert_index, expert_in, expert_out):
    rows, model = tokens.shape
    width = output_proj.shape[0]
    n_seq, n_ep = lax.axis_size("seq"), lax.axis_size("ep")
    seq, ep = lax.axis_index("seq"), lax.axis_index("ep")
    meta = jnp.stack([seq, ep]).astype(jnp.int32)
    own_rows = rows // n_ep
    experts = EXP_DEV * n_seq * n_ep // 2
    capacity = max(2, 2 * own_rows // experts)

    def over_seq(x, bits):
        return lax.ppermute(x, "seq", xor_pairs(n_seq, bits)) if bits else x

    def over_ep(x, bits):
        return lax.ppermute(x, "ep", xor_pairs(n_ep, bits)) if bits else x

    def exchange(outgoing, after=()):
        got = [over_seq(out, 2 * i) for i, out in reversed(list(enumerate(outgoing)))][::-1]
        got, after = lax.optimization_barrier((got, after))
        return got, over_seq(jnp.stack([g[1] for g in got]), 1)

    stacked = jnp.concatenate(
        [jnp.transpose(input_proj, (1, 2, 0)).reshape(3 * width, model), output_proj], axis=0
    )
    part = stacked.shape[0] // SPLIT
    along = [lax.dynamic_slice_in_dim(stacked, (seq % SPLIT) * part, part, 0)]
    for bit in range(n_ep.bit_length() - 1):
        along.append(over_ep(along[0], 1 << bit))

    own_sum, slots, space = attend_own(
        meta, tokens, stacked, expert_index, width, experts, capacity
    )
    along, own_sum = lax.optimization_barrier((along, own_sum))
    along = {0: along[0], **{1 << bit: a for bit, a in enumerate(along[1:])}}
    for m in range(1, n_ep):
        low = m & (m - 1)
        if low:
            along[m] = over_ep(along[low], m ^ low)

    def gather_layer(pieces):
        first = jnp.concatenate(pieces, axis=0)
        return [over_seq(first, bits) for bits in reversed(range(0, SPLIT, 2))][::-1]

    early = gather_layer([along[1], own_sum.reshape(-1, model)])
    later = [along[m] for m in range(2, n_ep)]
    later, early = lax.optimization_barrier((later, early))
    late = gather_layer(later)
    early = jnp.stack(early)
    early_other = over_seq(early, 1)

    sum_rows = own_sum.size // model
    sums = jnp.stack([early[:, -sum_rows:], early_other[:, -sum_rows:]], axis=1).reshape(SPLIT, HD, width)
    earlier = (jnp.arange(SPLIT) ^ (seq % SPLIT)) < seq % SPLIT
    prior = jnp.sum(jnp.where(earlier[:, None, None], sums.astype(F32), 0.0), axis=0)
    total, bit = jnp.sum(sums.astype(F32), axis=0), SPLIT
    while bit < n_seq:
        arrived = over_seq(total.astype(BF16), bit).astype(F32)
        prior = prior + jnp.where((seq & bit) != 0, arrived, 0.0)
        total, bit = total + arrived, 2 * bit
    index_rows = jnp.pad(
        expert_index.astype(BF16).reshape(own_rows // LANES, LANES), ((0, 4), (0, width - LANES))
    )
    prior = jnp.concatenate([prior.astype(BF16), index_rows], axis=0)
    priors = [prior]
    for m in range(1, n_ep):
        low = m & (m - 1)
        priors.append(over_ep(priors[low], m ^ low))

    early, prior = lax.optimization_barrier((early, prior))
    proj, space = attend_other(meta, space, early, early_other, 1, width, rows, model)
    projections = [output_proj, proj]
    late, projections, priors = lax.optimization_barrier((late, projections, priors))
    late = jnp.stack(late)
    late_other = over_seq(late, 1)
    def send(side, early_sum):
        return route(
            meta, space, late, late_other, projections, priors, side, early_sum, rows, n_seq, n_ep, capacity, experts
        )

    early_sum, *outgoing = send(1, None)
    stream, *outgoing_own = send(0, early_sum)
    got, crossed = exchange(outgoing, outgoing_own)
    outgoing_own, got = lax.optimization_barrier((outgoing_own, got))
    made, halves = [], []
    for local in range(EXP_DEV):
        if made:
            crossed, made = lax.optimization_barrier((crossed, made))
        made.append(expert(got, crossed, expert_in, expert_out, local)[0])
        cuts = jnp.split(made[-1][1], 1 + (local > 0))
        halves.append([over_ep(piece, 1) for piece in cuts])
    got, crossed = exchange(outgoing_own, ([half[0] for half in halves], made))
    owns, sides = [], []
    for local in range(EXP_DEV):
        if owns:
            crossed, owns = lax.optimization_barrier((crossed, owns))
        pair = (made[local][0], *halves[local])
        own, sums = expert(got, crossed, expert_in, expert_out, local, [pair])
        owns.append(own)
        sides.append([own[0], over_ep(own[1], 1), over_ep(sums[0], 2)])
    sides[0], owns = lax.optimization_barrier((sides[0], owns))
    total, returned, hots = stream, None, []
    for local in range(EXP_DEV):
        laid = lay_out(meta, *sides[local], n_seq, capacity)
        returned = exchange(laid, total if returned else sides[1:])
        last = local == EXP_DEV - 1
        hot = hots[local - 1] if local else None
        total, *found = combine(meta, total, slots, returned, hot, n_seq, n_ep, capacity, BF16 if last else F32)
        hots = hots or found
    return total


def solution(mesh):
    return jax.shard_map(
        per_device,
        mesh=mesh,
        in_specs=(
            P("seq", None),
            P(None, None, "ep"),
            P("ep", None),
            P(("seq", "ep"), None),
            P(("seq", "ep"), None, None),
            P(("seq", "ep"), None, None),
        ),
        out_specs=P(("seq", "ep"), None),
        check_vma=False,
    )
```
